512 devices in a mesh: seq: 64 (over x, y, z_lo), exp: 8 (over z_hi, core).
Axes of the slice: x: 4, y: 4, z: 16 (z_hi: 4, z_lo: 4; z = z_hi * 4 + z_lo), core: 2. Of those that a mesh axis runs over, the one named last changes fastest.
Arguments:
- queries: bfloat16 [64, 6144], P('seq', 'exp'), may hold values from -64 to 64
- key_cache: bfloat16 [49152, 1024], P('seq', 'exp'), may hold values from -6 to 6
- value_cache: bfloat16 [49152, 1024], P('seq', 'exp'), may hold values from -6 to 6
- key_new: bfloat16 [64, 1024], P('seq', 'exp'), may hold values from -16 to 16
- value_new: bfloat16 [64, 1024], P('seq', 'exp'), may hold values from -6 to 6
- window: int32 [1], replicated, may hold values from 6144 to 24575
- norm_gain: bfloat16 [6144], P('exp'), may hold values from 0.099609375 to 1.8984375
- expert_ids: int32 [64, 2], replicated, may hold values from 0 to 3, all different within a row; in each aligned block of 64 rows (0 to 63, 64 to 127, ...) at most 34 rows name the same one
- gate_values: float32 [64, 2], replicated, may hold values from 0.2 to 1
- w_gate: bfloat16 [6144, 65536], P(None, ('seq', 'exp')), may hold values from -0.078125 to 0.078125
- w_up: bfloat16 [6144, 65536], P(None, ('seq', 'exp')), may hold values from -0.078125 to 0.078125
- w_down: bfloat16 [65536, 6144], P(('seq', 'exp')), may hold values from -0.046875 to 0.046875
Outputs:
- mixed: bfloat16 [64, 6144], P('seq', 'exp')
The draws below stay inside these ranges and needn't reach their ends.
Inputs may be any that keep to these rules, and one draw needn't show every extreme that they name: `expert_ids`: the two ids of a token differ; every expert is named by at most 34 tokens, a bound that some block reaches.
All inputs are finite; a program needn't handle non-finite values.
Results may differ from the reference program's by a relative error of at most 0.038.
Values may be sent and summed in bfloat16 or wider, within the bound.
No kernel may reach another device: no remote copies, remote signals or barrier semaphores. Data moves between devices by JAX's collectives and lax.ppermute only.
A program may use at most 128 MiB of HBM per device.

```python
import math
import jax
import jax.numpy as jnp
import numpy as np
from jax import lax

D = 6144
HEADS = 48
KV_HEADS = 8
HD = 128
FF = 16384
EXPERTS = 4
Q_DEV = 1
CTX_DEV = 768
Q_TOK = 64
CTX = 49152
CAP = 34
N_SEQ = 64


def query_field(key, low, high):
    key = jax.random.fold_in(key, 11)
    base = jax.random.normal(key, (Q_TOK, HEADS * HD), jnp.float32)
    base = jnp.clip(base, -3.0, 3.0)
    factor = jax.random.uniform(jax.random.fold_in(key, 5), (Q_TOK, 1), jnp.float32, low, high)
    return base * factor


def draw_queries(key, part):
    field = query_field(key, 1.0, 1.0)
    return field.astype(jnp.bfloat16)


def draw_key_cache(key, part):
    key = jax.random.fold_in(key, 29)
    base = jnp.clip(jax.random.normal(key, (CTX, KV_HEADS * HD), jnp.float32), -6.0, 6.0)
    return base.astype(jnp.bfloat16)


def draw_key_new(key, part):
    own_key = jax.random.fold_in(key, 23)
    values = jnp.clip(jax.random.normal(own_key, (Q_TOK, KV_HEADS * HD), jnp.float32), -6.0, 6.0)
    return values.astype(jnp.bfloat16)


def levels(stream_key, dims, split, low, high):
    def one(position, shards_of):
        heights = jax.random.uniform(jax.random.fold_in(jax.random.fold_in(stream_key, 6), position), (shards_of,), jnp.float32, low / len(split), high / len(split))
        return jnp.repeat(jnp.exp(heights), dims[position] // shards_of).reshape((-1,) + (1,) * (len(dims) - position - 1))

    loudness = one(*split[0])
    for cut in split[1:]:
        loudness = loudness * one(*cut)
    return loudness


def shared_out(rng, own, number, rows, number_of, top, reach, lean):
    sequence = jax.random.permutation(rng, number_of)
    crowded, usual = shares(number_of, rows * top, reach, lean, True), shares(number_of, rows * top, reach, lean, False)
    places = jnp.arange(number_of)

    def named(lengths, offset_by):
        used = int((lengths > 0).sum())
        fixed = max(1, used // 4)
        moved = fixed + (places - fixed + offset_by * (used - fixed)) % max(1, number_of - fixed)
        return jnp.zeros((number_of,), jnp.int32).at[sequence[jnp.where(places < fixed, places, moved)]].set(jnp.asarray(lengths, jnp.int32))

    lengths = jnp.where(number % 4 == 0, named(crowded, number // 4), named(usual, number - number // 4 - 1))
    mixed = jax.random.permutation(jax.random.fold_in(own, 3), number_of)
    giver, sink = mixed[0:number_of // 2 * 2:2], mixed[1:number_of // 2 * 2:2]
    slack = jnp.minimum(lengths[giver] - 1, reach - lengths[sink]) // 2
    slack = jnp.where((giver == sequence[0]) | (sink == sequence[0]) | (lengths[sink] == 0), 0, jnp.maximum(slack, 0))
    moved = jax.random.randint(jax.random.fold_in(own, 4), (number_of // 2,), 0, 1 << 20) % (slack + 1)
    lengths = lengths.at[giver].add(-moved).at[sink].add(moved)
    labels = jnp.searchsorted(jnp.cumsum(lengths), jnp.arange(rows * top), side="right").astype(jnp.int32)
    grid = labels.reshape(top, rows).T
    grid = grid[jax.random.permutation(jax.random.fold_in(own, 1), rows)]
    offset_by = jax.random.randint(jax.random.fold_in(own, 2), (rows, 1), 0, top)
    return jnp.take_along_axis(grid, (jnp.arange(top)[None, :] + offset_by) % top, axis=1)


def shares(count, total, most, lean, full):
    weights = [(1 << 20) // math.isqrt(rank ** lean) + 1 for rank in range(1, count + 1)]
    largest = most if full else min(most, max(-(-total // count), total * weights[0] // sum(weights)))
    least = 1 if total - largest >= count - 1 else 0
    given, rest = [largest] + [least] * (count - 1), total - largest - least * (count - 1)
    while rest > 0:
        candidates = [i for i in range(1, count) if given[i] < largest] or [i for i in range(1, count) if given[i] < most]
        whole, left = sum([weights[i] for i in candidates]), rest
        for i in candidates:
            extra = min(most - given[i], max(1, left * weights[i] // whole), rest)
            given[i] = given[i] + extra
            rest = rest - extra
    return np.array(given)


def bell_draw(key, shape, scale, bound, cuts=(), held_as=jnp.bfloat16):
    result = scale * jax.random.normal(key, shape, jnp.float32)
    if cuts:
        result = result * levels(key, shape, cuts, -0.22, 0.18)
    return jnp.clip(result, -bound, bound).astype(held_as)


def setup_inputs(seed: int = 0) -> dict:
    keys = jax.random.split(jax.random.key(seed), 13)
    queries = draw_queries(jax.random.fold_in(keys[12], 71), 0)
    key_cache = draw_key_cache(jax.random.fold_in(keys[12], 71), 0)
    value_cache = bell_draw(keys[2], (CTX, KV_HEADS * HD), 1.0, 6.0, ((0, 64), (1, 8)))
    key_new = draw_key_new(jax.random.fold_in(keys[12], 71), 0)
    value_new = bell_draw(keys[4], (Q_TOK, KV_HEADS * HD), 1.0, 6.0, ((0, 64), (1, 8)))
    window = jax.random.randint(keys[5], (1,), CTX // 8, CTX // 2).astype(jnp.int32)
    norm_gain = jnp.clip(1.0 + 0.18 * jax.random.normal(keys[6], (D,), jnp.float32), 0.099609375, 1.8984375).astype(jnp.bfloat16)
    expert_ids_keys = jax.random.split(jax.random.fold_in(keys[7], 1), Q_TOK // Q_TOK)
    expert_ids_turns = jax.random.permutation(jax.random.fold_in(keys[7], 3), Q_TOK // Q_TOK)
    expert_ids = jax.vmap(lambda own, number: shared_out(jax.random.fold_in(keys[7], 2), own, number, Q_TOK, EXPERTS, 2, CAP, 2))(expert_ids_keys, expert_ids_turns).reshape((Q_TOK, 2))
    gate_values = jnp.clip(jax.random.uniform(keys[8], (Q_TOK, 2), jnp.float32, 0.2, 1.0), 0.2, 1.0)
    w_gate = bell_draw(keys[9], (D, EXPERTS * FF), D ** -0.5, 0.078125, ((1, 512),))
    w_up = bell_draw(keys[10], (D, EXPERTS * FF), D ** -0.5, 0.078125, ((1, 512),))
    w_down = bell_draw(keys[11], (EXPERTS * FF, D), FF ** -0.5, 0.046875, ((0, 512),))
    return {"queries": queries, "key_cache": key_cache, "value_cache": value_cache, "key_new": key_new, "value_new": value_new, "window": window, "norm_gain": norm_gain, "expert_ids": expert_ids, "gate_values": gate_values, "w_gate": w_gate, "w_up": w_up, "w_down": w_down}


ROPE_BASE = 1000000.0
NORM_EPS = 1e-05
MASKED = -1e+30

def frequencies(width):
    index = jnp.arange(width // 2, dtype=jnp.float32)
    return ROPE_BASE ** (-2.0 * index / width)

def rotate(values, angles):
    half = values.shape[-1] // 2
    first = values[..., :half]
    second = values[..., half:]
    cosine = jnp.cos(angles)
    sine = jnp.sin(angles)
    return jnp.concatenate([first * cosine - second * sine, second * cosine + first * sine], axis=-1)

def join_blocks(left, right):
    high = jnp.maximum(left[0], right[0])
    left_scale = jnp.exp(left[0] - high)
    right_scale = jnp.exp(right[0] - high)
    totals = left[1] * left_scale + right[1] * right_scale
    sums = left[2] * left_scale[..., None] + right[2] * right_scale[..., None]
    return (high, totals, sums)

def widen(values):
    return lax.optimization_barrier(values.astype(jnp.bfloat16)).astype(jnp.float32)

def reference(queries, key_cache, value_cache, key_new, value_new, window, norm_gain, expert_ids, gate_values, w_gate, w_up, w_down):
    group = HEADS // KV_HEADS
    freq = frequencies(HD)
    scale = HD ** (-0.5)
    limit = window[0]
    query_pos = CTX + jnp.arange(Q_TOK, dtype=jnp.int32)
    query_f32 = queries.astype(jnp.float32).reshape(Q_TOK, KV_HEADS, group, HD)
    near_query = widen(rotate(query_f32, query_pos.astype(jnp.float32)[:, None, None, None] * freq))
    far_query = widen(rotate(query_f32, limit.astype(jnp.float32) * freq))

    def block_step(carry, index):
        cache_keys = lax.dynamic_slice_in_dim(key_cache, index * CTX_DEV, CTX_DEV, 0)
        cache_values = lax.dynamic_slice_in_dim(value_cache, index * CTX_DEV, CTX_DEV, 0)
        fresh_keys = lax.dynamic_slice_in_dim(key_new, index * Q_DEV, Q_DEV, 0)
        fresh_values = lax.dynamic_slice_in_dim(value_new, index * Q_DEV, Q_DEV, 0)
        block_keys = jnp.concatenate([cache_keys, fresh_keys], 0).reshape(-1, KV_HEADS, HD).astype(jnp.float32)
        block_values = jnp.concatenate([cache_values, fresh_values], 0).reshape(-1, KV_HEADS, HD).astype(jnp.float32)
        key_pos = jnp.concatenate([index * CTX_DEV + jnp.arange(CTX_DEV, dtype=jnp.int32), CTX + index * Q_DEV + jnp.arange(Q_DEV, dtype=jnp.int32)]).astype(jnp.int32)
        rotated_keys = widen(rotate(block_keys, key_pos.astype(jnp.float32)[:, None, None] * freq))
        near = jnp.einsum('qkgd,pkd->kgqp', near_query, rotated_keys)
        far = jnp.einsum('qkgd,pkd->kgqp', far_query, block_keys)
        distance = query_pos[:, None] - key_pos[None, :]
        raw = jnp.where(distance < limit, near, far) * scale
        score = jnp.where(distance >= 0, raw, MASKED)
        block_max = lax.optimization_barrier(jnp.max(score, axis=-1))
        expo = jnp.exp(score - block_max[..., None])
        total = lax.optimization_barrier(jnp.sum(expo, axis=-1))
        block_sum = jnp.einsum('kgqp,pkd->kgqd', widen(expo), block_values)
        return (join_blocks(carry, (block_max, total, block_sum)), None)
    start = (jnp.full((KV_HEADS, group, Q_TOK), MASKED, jnp.float32), jnp.zeros((KV_HEADS, group, Q_TOK), jnp.float32), jnp.zeros((KV_HEADS, group, Q_TOK, HD), jnp.float32))
    merged, unused = lax.scan(block_step, start, jnp.arange(N_SEQ, dtype=jnp.int32))
    heads_out = merged[2] / merged[1][..., None]
    attention = jnp.transpose(heads_out, (2, 0, 1, 3)).reshape(Q_TOK, D).astype(jnp.bfloat16)
    attention_f32 = attention.astype(jnp.float32)
    mean_square = lax.optimization_barrier(jnp.mean(attention_f32 * attention_f32, axis=1))
    normed = (attention_f32 * lax.rsqrt(mean_square + NORM_EPS)[:, None] * norm_gain.astype(jnp.float32)).astype(jnp.bfloat16)
    combined = jnp.zeros((Q_TOK, D), jnp.float32)
    for expert in range(EXPERTS):
        gate = jnp.dot(normed, w_gate[:, expert * FF:(expert + 1) * FF], preferred_element_type=jnp.float32)
        upward = jnp.dot(normed, w_up[:, expert * FF:(expert + 1) * FF], preferred_element_type=jnp.float32)
        hidden = (jax.nn.silu(gate) * upward).astype(jnp.bfloat16)
        output = jnp.dot(hidden, w_down[expert * FF:(expert + 1) * FF, :], preferred_element_type=jnp.float32)
        share = lax.optimization_barrier(jnp.sum(jnp.where(expert_ids == expert, gate_values, jnp.zeros_like(gate_values)), axis=1))
        combined = combined + share[:, None] * output
    return (attention_f32 + combined).astype(jnp.bfloat16)
```

```python
import jax
import jax.numpy as jnp
from jax import lax
from jax.sharding import PartitionSpec as P

D = 6144
HEADS = 48
KV_HEADS = 8
HD = 128
FF = 16384


ROPE_BASE = 1000000.0
NORM_EPS = 1e-05
MASKED = -1e30


def frequencies(width):
    index = jnp.arange(width // 2, dtype=jnp.float32)
    return ROPE_BASE ** (-2.0 * index / width)


def rotate(values, angles):
    half = values.shape[-1] // 2
    first = values[..., :half]
    second = values[..., half:]
    cosine = jnp.cos(angles)
    sine = jnp.sin(angles)
    return jnp.concatenate(
        [first * cosine - second * sine, second * cosine + first * sine], axis=-1
    )


def head_scores(rotated_queries, block_keys):
    return jnp.einsum("qgd,pd->gqp", rotated_queries, block_keys, preferred_element_type=jnp.float32)


def swap(value, axis, mask):
    size = lax.axis_size(axis)
    return lax.ppermute(value, axis, [(i, i ^ mask) for i in range(size)])


def exchange(value, axis, groups=None):
    return lax.all_to_all(value, axis, 0, 0, axis_index_groups=groups, tiled=True)


def spread(value, axis, count, groups=None):
    return exchange(jnp.broadcast_to(value[None], (count, *value.shape)), axis, groups)


def near_groups(size, run):
    return [[run * i + j for j in range(run)] for i in range(size // run)]


def far_groups(size, run):
    return [[run * i + j for i in range(size // run)] for j in range(run)]


def local(
    queries,
    key_cache,
    value_cache,
    key_new,
    value_new,
    window,
    norm_gain,
    expert_ids,
    gate_values,
    w_gate,
    w_up,
    w_down,
):
    seq_count = lax.axis_size("seq")
    exp_count = lax.axis_size("exp")
    seq_at = lax.axis_index("seq")
    exp_at = lax.axis_index("exp")
    group = HEADS // KV_HEADS
    width = group * HD
    ctx_dev = key_cache.shape[0]
    q_tok = seq_count
    context = ctx_dev * seq_count
    freq = frequencies(HD)
    scale = HD ** (-0.5)
    limit = window[0]
    run = 8

    stretch = spread(queries.reshape(group, HD), "seq", run, near_groups(seq_count, run))
    stretch = spread(stretch, "seq", seq_count // run, far_groups(seq_count, run))
    stretch = stretch.reshape(q_tok, group, HD)
    query_pos = context + jnp.arange(q_tok, dtype=jnp.int32)
    query_f32 = stretch.astype(jnp.float32)
    near_query = rotate(
        query_f32, query_pos.astype(jnp.float32)[:, None, None] * freq
    ).astype(jnp.bfloat16)
    far_query = rotate(query_f32, limit.astype(jnp.float32) * freq).astype(jnp.bfloat16)
    key_pos = jnp.concatenate(
        [seq_at * ctx_dev + jnp.arange(ctx_dev, dtype=jnp.int32), context + seq_at[None]]
    )
    all_keys = jnp.concatenate([key_cache, key_new], 0)
    rotated_all = rotate(
        all_keys.astype(jnp.float32), key_pos.astype(jnp.float32)[:, None] * freq
    ).astype(jnp.bfloat16)
    distance = query_pos[:, None] - key_pos[None, :]
    near = head_scores(near_query, rotated_all)
    far = head_scores(far_query, all_keys)
    raw = jnp.where(distance < limit, near, far) * scale
    score = jnp.where(distance >= 0, raw, MASKED)
    block_max = jnp.max(score, axis=-1).astype(jnp.bfloat16)
    expo = jnp.exp(score - block_max.astype(jnp.float32)[..., None])
    total = jnp.sum(expo, axis=-1)
    block_values = jnp.concatenate([value_cache, value_new], 0)
    block_sum = jnp.einsum(
        "gqp,pd->qgd",
        expo.astype(jnp.bfloat16),
        block_values,
        preferred_element_type=jnp.float32,
    ).astype(jnp.bfloat16)
    total_high = total.astype(jnp.bfloat16)
    total_low = (total - total_high.astype(jnp.float32)).astype(jnp.bfloat16)
    extra = jnp.concatenate([block_max, total_high, total_low], 0).T
    extra = jnp.pad(extra, ((0, 0), (0, HD - 3 * group)))[:, None, :]
    parts = jnp.concatenate([block_sum, extra, jnp.zeros_like(extra)], 1)
    parts = exchange(parts, "seq")
    parts = parts.astype(jnp.float32)
    maxima = parts[:, group, :group]
    totals = parts[:, group, group : 2 * group] + parts[:, group, 2 * group : 3 * group]
    weights = jnp.exp(maxima - jnp.max(maxima, axis=0))
    below = jnp.sum(weights * totals, axis=0)
    above = jnp.sum(weights[:, :, None] * parts[:, :group, :], axis=0)
    attention = (above / below[:, None]).astype(jnp.bfloat16)

    ff_dev = w_gate.shape[1]
    expert = (seq_at * exp_count + exp_at) * ff_dev // FF
    capacity = (q_tok * 17 + 31) // 32
    matched = (expert_ids == expert).astype(jnp.int32)
    chosen = jnp.sum(matched, axis=1)
    weight = jnp.sum(gate_values * matched.astype(jnp.float32), axis=1)
    slot = jnp.cumsum(chosen) - chosen
    dispatch = (slot[None, :] == jnp.arange(capacity, dtype=jnp.int32)[:, None]) & (
        chosen[None, :] == 1
    )
    row_weight = jnp.sum(jnp.where(dispatch, weight[None, :], 0.0), axis=1)
    dispatch = dispatch.astype(jnp.bfloat16)

    tokens = spread(attention, "seq", seq_count).reshape(q_tok, width)
    routed = jnp.dot(dispatch, tokens, preferred_element_type=jnp.float32).astype(jnp.bfloat16)
    routed = jnp.concatenate([routed, norm_gain[None]], 0)

    piece = spread(routed, "exp", exp_count)
    piece = jnp.transpose(piece, (1, 0, 2)).reshape(capacity + 1, D)
    gain = piece[capacity].astype(jnp.float32)
    piece = piece[:capacity].astype(jnp.float32)
    squares = jnp.sum(piece * piece, axis=1)
    normed = (piece * lax.rsqrt(squares / D + NORM_EPS)[:, None] * gain).astype(jnp.bfloat16)
    gate = jnp.dot(normed, w_gate, preferred_element_type=jnp.float32)
    upward = jnp.dot(normed, w_up, preferred_element_type=jnp.float32)
    hidden = (jax.nn.silu(gate) * upward).astype(jnp.bfloat16)
    partial_value = jnp.dot(hidden, w_down, preferred_element_type=jnp.float32)

    core = exp_at % 2
    halves = partial_value.reshape(capacity, exp_count // 2, 2, width)
    kept = jnp.where(core == 0, halves[:, :, 0], halves[:, :, 1])
    sent = jnp.where(core == 0, halves[:, :, 1], halves[:, :, 0]).astype(jnp.bfloat16)
    half = kept + swap(sent, "exp", 1).astype(jnp.float32)
    half = jnp.transpose(half.astype(jnp.bfloat16), (1, 0, 2))
    quarters = exchange(half, "exp", far_groups(exp_count, 2))
    group_out = jnp.sum(quarters.astype(jnp.float32), axis=0)
    group_out = (group_out * row_weight[:, None]).astype(jnp.bfloat16)
    rows = jnp.dot(dispatch.T, group_out, preferred_element_type=jnp.float32).astype(jnp.bfloat16)
    rows = exchange(rows.reshape(q_tok, group, HD), "seq")
    expert_rows = jnp.sum(rows.astype(jnp.float32), axis=0)
    return (attention.astype(jnp.float32) + expert_rows).astype(jnp.bfloat16).reshape(1, width)


def solution(mesh):
    in_specs = (
        P("seq", "exp"),
        P("seq", "exp"),
        P("seq", "exp"),
        P("seq", "exp"),
        P("seq", "exp"),
        P(),
        P("exp"),
        P(),
        P(),
        P(None, ("seq", "exp")),
        P(None, ("seq", "exp")),
        P(("seq", "exp"), None),
    )
    out_specs = P("seq", "exp")
    return jax.shard_map(local, mesh=mesh, in_specs=in_specs, out_specs=out_specs, check_vma=False)
```

```python
import jax
import jax.numpy as jnp
from jax import lax
from jax.sharding import PartitionSpec as P

D = 6144
HEADS = 48
KV_HEADS = 8
HD = 128
FF = 16384


ROPE_BASE = 1000000.0
NORM_EPS = 1e-05
MASKED = -1e30


def frequencies(width):
    index = jnp.arange(width // 2, dtype=jnp.float32)
    return ROPE_BASE ** (-2.0 * index / width)


def rotate(values, angles):
    half = values.shape[-1] // 2
    first = values[..., :half]
    second = values[..., half:]
    cosine = jnp.cos(angles)
    sine = jnp.sin(angles)
    return jnp.concatenate(
        [first * cosine - second * sine, second * cosine + first * sine], axis=-1
    )


def head_scores(rotated_queries, block_keys):
    return jnp.einsum("qgd,pd->gqp", rotated_queries, block_keys, preferred_element_type=jnp.float32)


def swap(value, axis, mask):
    size = lax.axis_size(axis)
    return lax.ppermute(value, axis, [(i, i ^ mask) for i in range(size)])


def exchange(value, axis, groups=None):
    return lax.all_to_all(value, axis, 0, 0, axis_index_groups=groups, tiled=True)


def spread(value, axis, count, groups=None):
    return exchange(jnp.broadcast_to(value[None], (count, *value.shape)), axis, groups)


def local(
    queries,
    key_cache,
    value_cache,
    key_new,
    value_new,
    window,
    norm_gain,
    expert_ids,
    gate_values,
    w_gate,
    w_up,
    w_down,
):
    seq_count = lax.axis_size("seq")
    exp_count = lax.axis_size("exp")
    seq_at = lax.axis_index("seq")
    exp_at = lax.axis_index("exp")
    group = HEADS // KV_HEADS
    width = group * HD
    ctx_dev = key_cache.shape[0]
    q_tok = seq_count
    context = ctx_dev * seq_count
    freq = frequencies(HD)
    scale = HD ** (-0.5)
    limit = window[0]
    quarter = exp_count // 2
    core = exp_at % 2
    run = seq_count // 16
    plane = seq_count // run
    flat = [[run * i + j for i in range(plane)] for j in range(run)]
    tall = [
        [(run * i + j) * exp_count + 2 * h + c for j in range(run) for h in range(quarter)]
        for i in range(plane)
        for c in range(2)
    ]

    stretch = spread(queries.reshape(group, HD), "seq", seq_count)
    stretch, expert_ids, gate_values = lax.optimization_barrier(
        (stretch, expert_ids, gate_values)
    )
    query_pos = context + jnp.arange(q_tok, dtype=jnp.int32)
    query_f32 = stretch.astype(jnp.float32)
    near_query = rotate(
        query_f32, query_pos.astype(jnp.float32)[:, None, None] * freq
    ).astype(jnp.bfloat16)
    far_query = rotate(query_f32, limit.astype(jnp.float32) * freq).astype(jnp.bfloat16)
    key_pos = jnp.concatenate(
        [seq_at * ctx_dev + jnp.arange(ctx_dev, dtype=jnp.int32), context + seq_at[None]]
    )
    all_keys = jnp.concatenate([key_cache, key_new], 0)
    rotated_all = rotate(
        all_keys.astype(jnp.float32), key_pos.astype(jnp.float32)[:, None] * freq
    ).astype(jnp.bfloat16)
    distance = query_pos[:, None] - key_pos[None, :]
    near = head_scores(near_query, rotated_all)
    far = head_scores(far_query, all_keys)
    raw = jnp.where(distance < limit, near, far) * scale
    score = jnp.where(distance >= 0, raw, MASKED)
    block_max = jnp.max(score, axis=-1).astype(jnp.bfloat16)
    expo = jnp.exp(score - block_max.astype(jnp.float32)[..., None])
    total = jnp.sum(expo, axis=-1)
    block_values = jnp.concatenate([value_cache, value_new], 0)
    block_sum = jnp.einsum(
        "gqp,pd->qgd",
        expo.astype(jnp.bfloat16),
        block_values,
        preferred_element_type=jnp.float32,
    ).astype(jnp.bfloat16)
    total_high = total.astype(jnp.bfloat16)
    total_low = (total - total_high.astype(jnp.float32)).astype(jnp.bfloat16)
    extra = jnp.concatenate([block_max, total_high, total_low], 0).T
    extra = jnp.pad(extra, ((0, 0), (0, HD - 3 * group)))[:, None, :]
    parts = jnp.concatenate([block_sum, extra, jnp.zeros_like(extra)], 1)
    parts = exchange(parts.reshape(plane, run, group + 2, HD), "seq", flat)
    parts = parts.astype(jnp.float32)
    maxima = parts[:, :, group, :group]
    totals = parts[:, :, group, group : 2 * group] + parts[:, :, group, 2 * group : 3 * group]
    top = jnp.max(maxima, axis=0)
    weights = jnp.exp(maxima - top)
    total = jnp.sum(weights * totals, axis=0)
    sums = jnp.sum(weights[..., None] * parts[:, :, :group, :], axis=0).astype(jnp.bfloat16)
    total_high = total.astype(jnp.bfloat16)
    total_low = (total - total_high.astype(jnp.float32)).astype(jnp.bfloat16)
    facts = jnp.concatenate(
        [top.astype(jnp.bfloat16).ravel(), total_high.ravel(), total_low.ravel()]
    )
    facts = jnp.pad(facts, (0, HD - facts.shape[0]))[None]
    lines = jnp.concatenate(
        [
            sums.reshape(run * group, HD),
            facts,
            norm_gain.reshape(group, HD),
            jnp.zeros((1, HD), jnp.bfloat16),
        ]
    )
    lines = spread(lines, ("seq", "exp"), run * quarter, tall)
    lines = lines.reshape(run, quarter, -1, HD)
    gain = lines[0, :, run * group + 1 : run * group + 1 + group]
    facts = lines[:, :, run * group, : 3 * run * group].astype(jnp.float32)
    facts = facts.reshape(run, quarter, 3, run, group)
    weights = jnp.exp(facts[:, :, 0] - jnp.max(facts[:, :, 0], axis=0))
    below = jnp.sum(weights * (facts[:, :, 1] + facts[:, :, 2]), axis=0)
    sums = lines[:, :, : run * group].astype(jnp.float32).reshape(run, quarter, run, group, HD)
    above = jnp.sum(weights[..., None] * sums, axis=0)
    attention = (above / below[..., None]).astype(jnp.bfloat16)
    attention = jnp.transpose(attention, (1, 0, 2, 3))

    ff_dev = w_gate.shape[1]
    expert = (seq_at * exp_count + exp_at) * ff_dev // FF
    capacity = (q_tok * 17 + 31) // 32
    matched = (expert_ids == expert).astype(jnp.int32)
    chosen = jnp.sum(matched, axis=1)
    weight = jnp.sum(gate_values * matched.astype(jnp.float32), axis=1)
    slot = jnp.cumsum(chosen) - chosen
    dispatch = (slot[None, :] == jnp.arange(capacity, dtype=jnp.int32)[:, None]) & (
        chosen[None, :] == 1
    )
    row_weight = jnp.sum(jnp.where(dispatch, weight[None, :], 0.0), axis=1)
    dispatch = dispatch.astype(jnp.bfloat16)

    tokens = spread(attention.reshape(run, quarter * group, HD), "seq", plane, flat)
    tokens = tokens.reshape(q_tok, quarter * width)
    routed = jnp.dot(dispatch, tokens, preferred_element_type=jnp.float32).astype(jnp.bfloat16)
    mine = jnp.concatenate([routed, gain.reshape(1, quarter * width)], 0)
    other = swap(mine, "exp", 1)
    mine = mine.reshape(capacity + 1, quarter, width)
    other = other.reshape(capacity + 1, quarter, width)
    piece = jnp.stack(
        [jnp.where(core == 0, mine, other), jnp.where(core == 0, other, mine)], 2
    ).reshape(capacity + 1, D)
    gain = piece[capacity].astype(jnp.float32)
    piece = piece[:capacity].astype(jnp.float32)
    squares = jnp.sum(piece * piece, axis=1)
    normed = (piece * lax.rsqrt(squares / D + NORM_EPS)[:, None] * gain).astype(jnp.bfloat16)
    gate = jnp.dot(normed, w_gate, preferred_element_type=jnp.float32)
    upward = jnp.dot(normed, w_up, preferred_element_type=jnp.float32)
    hidden = (jax.nn.silu(gate) * upward).astype(jnp.bfloat16)
    partial_value = jnp.dot(hidden, w_down, preferred_element_type=jnp.float32)

    halves = partial_value.reshape(capacity, quarter, 2, width)
    kept = jnp.where(core == 0, halves[:, :, 0], halves[:, :, 1])
    sent = jnp.where(core == 0, halves[:, :, 1], halves[:, :, 0]).astype(jnp.bfloat16)
    half = kept + swap(sent, "exp", 1).astype(jnp.float32)
    half = (half.reshape(capacity, quarter * width) * row_weight[:, None]).astype(jnp.bfloat16)
    rows = jnp.dot(dispatch.T, half, preferred_element_type=jnp.float32).astype(jnp.bfloat16)
    rows = exchange(rows.reshape(plane, run, quarter * group, HD), "seq", flat)
    rows = jnp.sum(rows.astype(jnp.float32), axis=0).astype(jnp.bfloat16)
    rows = exchange(rows.reshape(run * quarter, group, HD), ("seq", "exp"), tall)
    expert_rows = jnp.sum(rows.astype(jnp.float32), axis=0)
    own = attention.reshape(run * quarter, group, HD)
    own = lax.dynamic_index_in_dim(own, seq_at % run * quarter + exp_at // 2, 0, False)
    return (own.astype(jnp.float32) + expert_rows).astype(jnp.bfloat16).reshape(1, width)


def solution(mesh):
    in_specs = (
        P("seq", "exp"),
        P("seq", "exp"),
        P("seq", "exp"),
        P("seq", "exp"),
        P("seq", "exp"),
        P(),
        P("exp"),
        P(),
        P(),
        P(None, ("seq", "exp")),
        P(None, ("seq", "exp")),
        P(("seq", "exp"), None),
    )
    out_specs = P("seq", "exp")
    return jax.shard_map(local, mesh=mesh, in_specs=in_specs, out_specs=out_specs, check_vma=False)
```

```python
import functools

import jax
import jax.numpy as jnp
from jax import lax
from jax.experimental import pallas as pl
from jax.experimental.pallas import tpu as pltpu
from jax.sharding import PartitionSpec as P

D = 6144
HEADS = 48
KV_HEADS = 8
HD = 128
FF = 16384


ROPE_BASE = 1000000.0
NORM_EPS = 1e-05
MASKED = -1e30


def frequencies(width):
    index = jnp.arange(width // 2, dtype=jnp.float32)
    return ROPE_BASE ** (-2.0 * index / width)


def rotate(values, angles):
    half = values.shape[-1] // 2
    first = values[..., :half]
    second = values[..., half:]
    cosine = jnp.cos(angles)
    sine = jnp.sin(angles)
    return jnp.concatenate(
        [first * cosine - second * sine, second * cosine + first * sine], axis=-1
    )


def dot(left, right):
    return jnp.dot(left, right, preferred_element_type=jnp.float32)


def dot_rows(left, right):
    return lax.dot_general(
        left, right, (((1,), (1,)), ((), ())), preferred_element_type=jnp.float32
    )


def copies_kernel(row_ref, out_ref):
    group = out_ref.shape[1]
    row = row_ref[...].astype(jnp.float32)
    block = jnp.concatenate([row[:, h * HD : (h + 1) * HD] for h in range(group)], 0)
    out_ref[...] = jnp.broadcast_to(block[None], out_ref.shape).astype(out_ref.dtype)


def row_copies(row, count, group):
    return pl.pallas_call(
        copies_kernel,
        out_shape=jax.ShapeDtypeStruct((count, group, HD), row.dtype),
    )(row)


def attend_kernel(
    context,
    place_ref,
    near_ref,
    far_ref,
    rotated_ref,
    keys_ref,
    values_ref,
    fresh_rotated_ref,
    fresh_key_ref,
    fresh_value_ref,
    out_ref,
    wide_ref,
):
    q_tok = out_ref.shape[0]
    rows, ctx_dev = near_ref.shape[0], keys_ref.shape[0]
    group = rows // q_tok
    scale = HD ** (-0.5)
    start, limit, seq_at = place_ref[0], place_ref[1], place_ref[2]
    near_query = near_ref[...]
    far_query = far_ref[...]
    token = lax.broadcasted_iota(jnp.int32, (rows, ctx_dev), 0) & (q_tok - 1)
    key_pos = start + lax.broadcasted_iota(jnp.int32, (rows, ctx_dev), 1)
    distance = context + token - key_pos
    near = dot_rows(near_query, rotated_ref[...])
    far = dot_rows(far_query, keys_ref[...])
    score = jnp.where(distance < limit, near, far) * scale
    distance = (lax.broadcasted_iota(jnp.int32, (rows, 1), 0) & (q_tok - 1)) - seq_at
    fresh_rotated = fresh_rotated_ref[...].astype(jnp.float32)
    fresh_key = fresh_key_ref[...].astype(jnp.float32)
    near = jnp.sum(near_query.astype(jnp.float32) * fresh_rotated, axis=1, keepdims=True)
    far = jnp.sum(far_query.astype(jnp.float32) * fresh_key, axis=1, keepdims=True)
    fresh = jnp.where(distance < limit, near, far) * scale
    fresh = jnp.where(distance >= 0, fresh, MASKED)
    high = jnp.maximum(jnp.max(score, axis=1, keepdims=True), fresh)
    high = high.astype(jnp.bfloat16).astype(jnp.float32)
    expo = jnp.exp(score - high)
    fresh = jnp.exp(fresh - high)
    total = jnp.sum(expo, axis=1, keepdims=True) + fresh
    sums = dot(expo.astype(jnp.bfloat16), values_ref[...])
    fresh = fresh.astype(jnp.bfloat16).astype(jnp.float32)
    sums = sums + fresh * fresh_value_ref[...].astype(jnp.float32)
    total_high = total.astype(jnp.bfloat16).astype(jnp.float32)
    total_low = total - total_high
    lane = lax.broadcasted_iota(jnp.int32, (q_tok, HD), 1)
    facts = jnp.zeros((q_tok, HD), jnp.float32)
    for h in range(group):
        part = slice(h * q_tok, (h + 1) * q_tok)
        wide_ref[:, h, :] = sums[part]
        facts = jnp.where(lane == h, high[part], facts)
        facts = jnp.where(lane == group + h, total_high[part], facts)
        facts = jnp.where(lane == 2 * group + h, total_low[part], facts)
    wide_ref[:, group, :] = facts
    wide_ref[:, group + 1, :] = jnp.zeros((q_tok, HD), jnp.float32)
    out_ref[...] = wide_ref[...].astype(out_ref.dtype)


def attend(context, q_tok, place, *arrays):
    rows = arrays[0].shape[0] // q_tok + 2
    vmem = pl.BlockSpec(memory_space=pltpu.VMEM)
    return pl.pallas_call(
        functools.partial(attend_kernel, context),
        out_shape=jax.ShapeDtypeStruct((q_tok, rows, HD), jnp.bfloat16),
        in_specs=[pl.BlockSpec(memory_space=pltpu.SMEM)] + [vmem] * len(arrays),
        out_specs=vmem,
        scratch_shapes=[pltpu.VMEM((q_tok, rows, HD), jnp.float32)],
        compiler_params=pltpu.CompilerParams(vmem_limit_bytes=32 << 20),
    )(place, *arrays)


def expert_kernel(
    gain_row,
    place_ref,
    mine_ref,
    other_ref,
    w_gate,
    w_up,
    w_down,
    kept_ref,
    sent_ref,
    gate_ref,
    up_ref,
    down_ref,
    sems,
):
    rows, half = mine_ref.shape
    depth = w_gate.shape[0]
    steps = 4
    width = half // steps
    core = place_ref[0]
    copies = []
    for i in range(steps):
        part = pl.ds(i * (depth // steps), depth // steps)
        for j, (source, target) in enumerate(((w_gate, gate_ref), (w_up, up_ref))):
            copy = pltpu.make_async_copy(source.at[part], target.at[part], sems.at[2 * i + j])
            copy.start()
            copies.append(copy)
    last = pltpu.make_async_copy(w_down, down_ref, sems.at[2 * steps])
    last.start()

    mine = mine_ref[...].astype(jnp.float32)
    other = other_ref[...].astype(jnp.float32)
    squares = jnp.sum(mine * mine, axis=1, keepdims=True)
    squares = squares + jnp.sum(other * other, axis=1, keepdims=True)
    scale = lax.rsqrt(squares / D + NORM_EPS)
    mine = (mine * scale * mine[gain_row : gain_row + 1]).astype(jnp.bfloat16)
    other = (other * scale * other[gain_row : gain_row + 1]).astype(jnp.bfloat16)
    gate = jnp.zeros((rows, gate_ref.shape[1]), jnp.float32)
    upward = gate
    for i in range(steps):
        copies[2 * i].wait()
        copies[2 * i + 1].wait()
        for side, values in ((core, mine), (1 - core, other)):
            part = pl.ds(pl.multiple_of((2 * i + side) * width, width), width)
            block = values[:, i * width : (i + 1) * width]
            gate = gate + dot(block, gate_ref[part, :])
            upward = upward + dot(block, up_ref[part, :])
    hidden = (gate / (1.0 + jnp.exp(-gate)) * upward).astype(jnp.bfloat16)
    last.wait()
    for i in range(steps):
        part = pl.ds(pl.multiple_of((2 * i + 1 - core) * width, width), width)
        columns = slice(i * width, (i + 1) * width)
        sent_ref[:, columns] = dot(hidden, down_ref[:, part]).astype(sent_ref.dtype)
        part = pl.ds(pl.multiple_of((2 * i + core) * width, width), width)
        kept_ref[:, columns] = dot(hidden, down_ref[:, part])


def feed(gain_row, place, mine, other, w_gate, w_up, w_down):
    vmem = pl.BlockSpec(memory_space=pltpu.VMEM)
    anywhere = pl.BlockSpec(memory_space=pl.ANY)
    return pl.pallas_call(
        functools.partial(expert_kernel, gain_row),
        out_shape=(
            jax.ShapeDtypeStruct(mine.shape, jnp.float32),
            jax.ShapeDtypeStruct(mine.shape, jnp.bfloat16),
        ),
        in_specs=[pl.BlockSpec(memory_space=pltpu.SMEM), vmem, vmem] + [anywhere] * 3,
        out_specs=(vmem, vmem),
        scratch_shapes=[
            pltpu.VMEM(w_gate.shape, w_gate.dtype),
            pltpu.VMEM(w_up.shape, w_up.dtype),
            pltpu.VMEM(w_down.shape, w_down.dtype),
            pltpu.SemaphoreType.DMA((9,)),
        ],
        compiler_params=pltpu.CompilerParams(vmem_limit_bytes=32 << 20),
    )(place, mine, other, w_gate, w_up, w_down)


def swap(value, axis, mask):
    size = lax.axis_size(axis)
    return lax.ppermute(value, axis, [(i, i ^ mask) for i in range(size)])


def exchange(value, axis, groups=None):
    return lax.all_to_all(value, axis, 0, 0, axis_index_groups=groups, tiled=True)


def spread(value, axis, count, groups=None):
    return exchange(jnp.broadcast_to(value[None], (count, *value.shape)), axis, groups)


def local(
    queries,
    key_cache,
    value_cache,
    key_new,
    value_new,
    window,
    norm_gain,
    expert_ids,
    gate_values,
    w_gate,
    w_up,
    w_down,
):
    seq_count = lax.axis_size("seq")
    exp_count = lax.axis_size("exp")
    seq_at = lax.axis_index("seq")
    exp_at = lax.axis_index("exp")
    group = HEADS // KV_HEADS
    width = group * HD
    ctx_dev = key_cache.shape[0]
    q_tok = seq_count
    context = ctx_dev * seq_count
    freq = frequencies(HD)
    limit = window[0]
    quarter = exp_count // 2
    core = exp_at % 2
    run = seq_count // 16
    plane = seq_count // run
    flat = [[run * i + j for i in range(plane)] for j in range(run)]
    tall = [
        [(run * i + j) * exp_count + 2 * h + c for j in range(run) for h in range(quarter)]
        for i in range(plane)
        for c in range(2)
    ]

    stretch = exchange(row_copies(queries, seq_count, group), "seq")
    stretch, expert_ids, gate_values = lax.optimization_barrier(
        (stretch, expert_ids, gate_values)
    )
    query_pos = context + jnp.arange(q_tok, dtype=jnp.int32)
    query_f32 = stretch.astype(jnp.float32)
    near_query = rotate(
        query_f32, query_pos.astype(jnp.float32)[:, None, None] * freq
    ).astype(jnp.bfloat16)
    far_query = rotate(query_f32, limit.astype(jnp.float32) * freq).astype(jnp.bfloat16)
    near_query = jnp.transpose(near_query, (1, 0, 2)).reshape(group * q_tok, HD)
    far_query = jnp.transpose(far_query, (1, 0, 2)).reshape(group * q_tok, HD)
    key_pos = seq_at * ctx_dev + jnp.arange(ctx_dev, dtype=jnp.int32)
    rotated_cache = rotate(
        key_cache.astype(jnp.float32), key_pos.astype(jnp.float32)[:, None] * freq
    ).astype(jnp.bfloat16)
    rotated_fresh = rotate(
        key_new.astype(jnp.float32), (context + seq_at).astype(jnp.float32) * freq
    ).astype(jnp.bfloat16)
    place = jnp.stack([seq_at * ctx_dev, limit, seq_at])
    parts = attend(
        context,
        q_tok,
        place,
        near_query,
        far_query,
        rotated_cache,
        key_cache,
        value_cache,
        rotated_fresh,
        key_new,
        value_new,
    )

    parts = exchange(parts.reshape(plane, run, group + 2, HD), "seq", flat)
    parts = parts.astype(jnp.float32)
    maxima = parts[:, :, group, :group]
    totals = parts[:, :, group, group : 2 * group] + parts[:, :, group, 2 * group : 3 * group]
    top = jnp.max(maxima, axis=0)
    weights = jnp.exp(maxima - top)
    total = jnp.sum(weights * totals, axis=0)
    sums = jnp.sum(weights[..., None] * parts[:, :, :group, :], axis=0).astype(jnp.bfloat16)
    total_high = total.astype(jnp.bfloat16)
    total_low = (total - total_high.astype(jnp.float32)).astype(jnp.bfloat16)
    facts = jnp.concatenate(
        [top.astype(jnp.bfloat16).ravel(), total_high.ravel(), total_low.ravel()]
    )
    facts = jnp.pad(facts, (0, HD - facts.shape[0]))[None]
    lines = jnp.concatenate(
        [
            sums.reshape(run * group, HD),
            facts,
            norm_gain.reshape(group, HD),
            jnp.zeros((1, HD), jnp.bfloat16),
        ]
    )
    lines = spread(lines, ("seq", "exp"), run * quarter, tall)
    lines = lines.reshape(run, quarter, -1, HD)
    gain = lines[0, :, run * group + 1 : run * group + 1 + group]
    facts = lines[:, :, run * group, : 3 * run * group].astype(jnp.float32)
    facts = facts.reshape(run, quarter, 3, run, group)
    weights = jnp.exp(facts[:, :, 0] - jnp.max(facts[:, :, 0], axis=0))
    below = jnp.sum(weights * (facts[:, :, 1] + facts[:, :, 2]), axis=0)
    sums = lines[:, :, : run * group].astype(jnp.float32).reshape(run, quarter, run, group, HD)
    above = jnp.sum(weights[..., None] * sums, axis=0)
    attention = (above / below[..., None]).astype(jnp.bfloat16)
    attention = jnp.transpose(attention, (1, 0, 2, 3))

    ff_dev = w_gate.shape[1]
    expert = (seq_at * exp_count + exp_at) * ff_dev // FF
    capacity = (q_tok * 17 + 31) // 32
    matched = (expert_ids == expert).astype(jnp.int32)
    chosen = jnp.sum(matched, axis=1)
    weight = jnp.sum(gate_values * matched.astype(jnp.float32), axis=1)
    slot = jnp.cumsum(chosen) - chosen
    gain_row = -(-capacity // 8) * 8
    rows = jnp.arange(-(-(gain_row + 1) // 16) * 16, dtype=jnp.int32)[:, None]
    dispatch = (slot[None, :] == rows) & (rows < capacity) & (
        chosen[None, :] == 1
    )
    row_weight = jnp.sum(jnp.where(dispatch, weight[None, :], 0.0), axis=1)
    dispatch = dispatch.astype(jnp.bfloat16)

    tokens = spread(attention.reshape(run, quarter * group, HD), "seq", plane, flat)
    tokens = tokens.reshape(q_tok, quarter * width)
    routed = dot(dispatch, tokens)
    mine = jnp.where(rows == gain_row, gain.reshape(1, -1).astype(jnp.float32), routed)
    mine = mine.astype(jnp.bfloat16)
    other = swap(mine, "exp", 1)
    kept, sent = feed(gain_row, core[None], mine, other, w_gate, w_up, w_down)

    half = kept + swap(sent, "exp", 1).astype(jnp.float32)
    half = (half * row_weight[:, None]).astype(jnp.bfloat16)
    rows = jnp.dot(dispatch.T, half, preferred_element_type=jnp.float32).astype(jnp.bfloat16)
    rows = exchange(rows.reshape(plane, run, quarter * group, HD), "seq", flat)
    rows = jnp.sum(rows.astype(jnp.float32), axis=0).astype(jnp.bfloat16)
    rows = exchange(rows.reshape(run * quarter, group, HD), ("seq", "exp"), tall)
    expert_rows = jnp.sum(rows.astype(jnp.float32), axis=0)
    own = attention.reshape(run * quarter, group, HD)
    own = lax.dynamic_index_in_dim(own, seq_at % run * quarter + exp_at // 2, 0, False)
    return (own.astype(jnp.float32) + expert_rows).astype(jnp.bfloat16).reshape(1, width)


def solution(mesh):
    in_specs = (
        P("seq", "exp"),
        P("seq", "exp"),
        P("seq", "exp"),
        P("seq", "exp"),
        P("seq", "exp"),
        P(),
        P("exp"),
        P(),
        P(),
        P(None, ("seq", "exp")),
        P(None, ("seq", "exp")),
        P(("seq", "exp"), None),
    )
    out_specs = P("seq", "exp")
    return jax.shard_map(local, mesh=mesh, in_specs=in_specs, out_specs=out_specs, check_vma=False)
```

```python
import functools

import jax
import jax.numpy as jnp
from jax import lax
from jax.experimental import pallas as pl
from jax.experimental.pallas import tpu as pltpu
from jax.sharding import PartitionSpec as P

D = 6144
HEADS = 48
KV_HEADS = 8
HD = 128
FF = 16384


ROPE_BASE = 1000000.0
NORM_EPS = 1e-05
MASKED = -1e30


def frequencies(width):
    index = jnp.arange(width // 2, dtype=jnp.float32)
    return ROPE_BASE ** (-2.0 * index / width)


def rotate(values, angles):
    half = values.shape[-1] // 2
    first = values[..., :half]
    second = values[..., half:]
    cosine = jnp.cos(angles)
    sine = jnp.sin(angles)
    return jnp.concatenate(
        [first * cosine - second * sine, second * cosine + first * sine], axis=-1
    )


def dot(left, right):
    return jnp.dot(left, right, preferred_element_type=jnp.float32)


def dot_rows(left, right):
    return lax.dot_general(
        left, right, (((1,), (1,)), ((), ())), preferred_element_type=jnp.float32
    )


def copies_kernel(row_ref, out_ref):
    group = out_ref.shape[1]
    row = row_ref[...].astype(jnp.float32)
    block = jnp.concatenate([row[:, h * HD : (h + 1) * HD] for h in range(group)], 0)
    out_ref[...] = jnp.broadcast_to(block[None], out_ref.shape).astype(out_ref.dtype)


def row_copies(row, count, group):
    return pl.pallas_call(
        copies_kernel,
        out_shape=jax.ShapeDtypeStruct((count, group, HD), row.dtype),
    )(row)


def attend_kernel(
    context,
    place_ref,
    near_ref,
    far_ref,
    rotated_ref,
    keys_ref,
    values_ref,
    fresh_rotated_ref,
    fresh_key_ref,
    fresh_value_ref,
    out_ref,
    wide_ref,
):
    q_tok = out_ref.shape[0]
    rows, ctx_dev = near_ref.shape[0], keys_ref.shape[0]
    group = rows // q_tok
    scale = HD ** (-0.5)
    start, limit, seq_at = place_ref[0], place_ref[1], place_ref[2]
    near_query = near_ref[...]
    far_query = far_ref[...]
    token = lax.broadcasted_iota(jnp.int32, (rows, ctx_dev), 0) & (q_tok - 1)
    key_pos = start + lax.broadcasted_iota(jnp.int32, (rows, ctx_dev), 1)
    distance = context + token - key_pos
    near = dot_rows(near_query, rotated_ref[...])
    far = dot_rows(far_query, keys_ref[...])
    score = jnp.where(distance < limit, near, far) * scale
    distance = (lax.broadcasted_iota(jnp.int32, (rows, 1), 0) & (q_tok - 1)) - seq_at
    fresh_rotated = fresh_rotated_ref[...].astype(jnp.float32)
    fresh_key = fresh_key_ref[...].astype(jnp.float32)
    near = jnp.sum(near_query.astype(jnp.float32) * fresh_rotated, axis=1, keepdims=True)
    far = jnp.sum(far_query.astype(jnp.float32) * fresh_key, axis=1, keepdims=True)
    fresh = jnp.where(distance < limit, near, far) * scale
    fresh = jnp.where(distance >= 0, fresh, MASKED)
    high = jnp.maximum(jnp.max(score, axis=1, keepdims=True), fresh)
    high = high.astype(jnp.bfloat16).astype(jnp.float32)
    expo = jnp.exp(score - high)
    fresh = jnp.exp(fresh - high)
    total = jnp.sum(expo, axis=1, keepdims=True) + fresh
    sums = dot(expo.astype(jnp.bfloat16), values_ref[...])
    fresh = fresh.astype(jnp.bfloat16).astype(jnp.float32)
    sums = sums + fresh * fresh_value_ref[...].astype(jnp.float32)
    total_high = total.astype(jnp.bfloat16).astype(jnp.float32)
    total_low = total - total_high
    lane = lax.broadcasted_iota(jnp.int32, (q_tok, HD), 1)
    facts = jnp.zeros((q_tok, HD), jnp.float32)
    for h in range(group):
        part = slice(h * q_tok, (h + 1) * q_tok)
        wide_ref[:, h, :] = sums[part]
        facts = jnp.where(lane == h, high[part], facts)
        facts = jnp.where(lane == group + h, total_high[part], facts)
        facts = jnp.where(lane == 2 * group + h, total_low[part], facts)
    wide_ref[:, group, :] = facts
    wide_ref[:, group + 1, :] = jnp.zeros((q_tok, HD), jnp.float32)
    out_ref[...] = wide_ref[...].astype(out_ref.dtype)


def attend(context, q_tok, place, *arrays):
    rows = arrays[0].shape[0] // q_tok + 2
    vmem = pl.BlockSpec(memory_space=pltpu.VMEM)
    return pl.pallas_call(
        functools.partial(attend_kernel, context),
        out_shape=jax.ShapeDtypeStruct((q_tok, rows, HD), jnp.bfloat16),
        in_specs=[pl.BlockSpec(memory_space=pltpu.SMEM)] + [vmem] * len(arrays),
        out_specs=vmem,
        scratch_shapes=[pltpu.VMEM((q_tok, rows, HD), jnp.float32)],
        compiler_params=pltpu.CompilerParams(vmem_limit_bytes=16 << 20),
    )(place, *arrays)


def expert_kernel(
    gain_row,
    place_ref,
    mine_ref,
    other_ref,
    gate_ref,
    up_ref,
    down_ref,
    kept_ref,
    sent_ref,
):
    rows, half = mine_ref.shape
    steps = 4
    width = half // steps
    core = place_ref[0]
    mine = mine_ref[...].astype(jnp.float32)
    other = other_ref[...].astype(jnp.float32)
    squares = jnp.sum(mine * mine, axis=1, keepdims=True)
    squares = squares + jnp.sum(other * other, axis=1, keepdims=True)
    scale = lax.rsqrt(squares / D + NORM_EPS)
    mine = (mine * scale * mine[gain_row : gain_row + 1]).astype(jnp.bfloat16)
    other = (other * scale * other[gain_row : gain_row + 1]).astype(jnp.bfloat16)
    gate = jnp.zeros((rows, gate_ref.shape[1]), jnp.float32)
    upward = gate
    for i in range(steps):
        for side, values in ((core, mine), (1 - core, other)):
            part = pl.ds(pl.multiple_of((2 * i + side) * width, width), width)
            block = values[:, i * width : (i + 1) * width]
            gate = gate + dot(block, gate_ref[part, :])
            upward = upward + dot(block, up_ref[part, :])
    hidden = (gate / (1.0 + jnp.exp(-gate)) * upward).astype(jnp.bfloat16)
    for i in range(steps):
        part = pl.ds(pl.multiple_of((2 * i + 1 - core) * width, width), width)
        columns = slice(i * width, (i + 1) * width)
        sent_ref[:, columns] = dot(hidden, down_ref[:, part]).astype(sent_ref.dtype)
        part = pl.ds(pl.multiple_of((2 * i + core) * width, width), width)
        kept_ref[:, columns] = dot(hidden, down_ref[:, part])


def feed(gain_row, place, mine, other, w_gate, w_up, w_down):
    vmem = pl.BlockSpec(memory_space=pltpu.VMEM)
    return pl.pallas_call(
        functools.partial(expert_kernel, gain_row),
        out_shape=(
            jax.ShapeDtypeStruct(mine.shape, jnp.float32),
            jax.ShapeDtypeStruct(mine.shape, jnp.bfloat16),
        ),
        in_specs=[pl.BlockSpec(memory_space=pltpu.SMEM)] + [vmem] * 5,
        out_specs=(vmem, vmem),
        compiler_params=pltpu.CompilerParams(vmem_limit_bytes=16 << 20),
    )(place, mine, other, w_gate, w_up, w_down)


def swap(value, axis, mask):
    size = lax.axis_size(axis)
    return lax.ppermute(value, axis, [(i, i ^ mask) for i in range(size)])


def exchange(value, axis, groups=None):
    return lax.all_to_all(value, axis, 0, 0, axis_index_groups=groups, tiled=True)


def spread(value, axis, count, groups=None):
    return exchange(jnp.broadcast_to(value[None], (count, *value.shape)), axis, groups)


def local(
    queries,
    key_cache,
    value_cache,
    key_new,
    value_new,
    window,
    norm_gain,
    expert_ids,
    gate_values,
    w_gate,
    w_up,
    w_down,
):
    seq_count = lax.axis_size("seq")
    exp_count = lax.axis_size("exp")
    seq_at = lax.axis_index("seq")
    exp_at = lax.axis_index("exp")
    group = HEADS // KV_HEADS
    width = group * HD
    ctx_dev = key_cache.shape[0]
    q_tok = seq_count
    context = ctx_dev * seq_count
    freq = frequencies(HD)
    limit = window[0]
    quarter = exp_count // 2
    core = exp_at % 2
    run = seq_count // 16
    plane = seq_count // run
    flat = [[run * i + j for i in range(plane)] for j in range(run)]
    tall = [
        [(run * i + j) * exp_count + 2 * h + c for j in range(run) for h in range(quarter)]
        for i in range(plane)
        for c in range(2)
    ]

    stretch = exchange(row_copies(queries, seq_count, group), "seq")
    stretch, expert_ids, gate_values = lax.optimization_barrier(
        (stretch, expert_ids, gate_values)
    )
    query_pos = context + jnp.arange(q_tok, dtype=jnp.int32)
    query_f32 = stretch.astype(jnp.float32)
    near_query = rotate(
        query_f32, query_pos.astype(jnp.float32)[:, None, None] * freq
    ).astype(jnp.bfloat16)
    far_query = rotate(query_f32, limit.astype(jnp.float32) * freq).astype(jnp.bfloat16)
    near_query = jnp.transpose(near_query, (1, 0, 2)).reshape(group * q_tok, HD)
    far_query = jnp.transpose(far_query, (1, 0, 2)).reshape(group * q_tok, HD)
    key_pos = seq_at * ctx_dev + jnp.arange(ctx_dev, dtype=jnp.int32)
    rotated_cache = rotate(
        key_cache.astype(jnp.float32), key_pos.astype(jnp.float32)[:, None] * freq
    ).astype(jnp.bfloat16)
    rotated_fresh = rotate(
        key_new.astype(jnp.float32), (context + seq_at).astype(jnp.float32) * freq
    ).astype(jnp.bfloat16)
    place = jnp.stack([seq_at * ctx_dev, limit, seq_at])
    parts = attend(
        context,
        q_tok,
        place,
        near_query,
        far_query,
        rotated_cache,
        key_cache,
        value_cache,
        rotated_fresh,
        key_new,
        value_new,
    )

    parts = exchange(parts, "seq").astype(jnp.float32)
    maxima = parts[:, group, :group]
    totals = parts[:, group, group : 2 * group] + parts[:, group, 2 * group : 3 * group]
    weights = jnp.exp(maxima - jnp.max(maxima, axis=0))
    below = jnp.sum(weights * totals, axis=0)
    above = jnp.sum(weights[:, :, None] * parts[:, :group, :], axis=0)
    attention = (above / below[:, None]).astype(jnp.bfloat16)

    share = width // run
    share_rows = -(-share // HD)
    gain = lax.dynamic_slice_in_dim(norm_gain, seq_at % run * share, share)
    gain = jnp.pad(gain, (0, share_rows * HD - share)).reshape(share_rows, HD)
    lines = spread(jnp.concatenate([attention, gain]), ("seq", "exp"), run * quarter, tall)
    lines = lines.reshape(run, quarter, group + share_rows, HD)
    gain = lines[:, :, group:].reshape(run, quarter, share_rows * HD)[:, :, :share]
    gain = jnp.transpose(gain, (1, 0, 2)).reshape(1, quarter * width)
    lines = lines[:, :, :group].reshape(run, quarter * group, HD)

    ff_dev = w_gate.shape[1]
    expert = (seq_at * exp_count + exp_at) * ff_dev // FF
    capacity = (q_tok * 17 + 31) // 32
    matched = (expert_ids == expert).astype(jnp.int32)
    chosen = jnp.sum(matched, axis=1)
    weight = jnp.sum(gate_values * matched.astype(jnp.float32), axis=1)
    slot = jnp.cumsum(chosen) - chosen
    gain_row = -(-capacity // 8) * 8
    rows = jnp.arange(-(-(gain_row + 1) // 16) * 16, dtype=jnp.int32)[:, None]
    dispatch = (slot[None, :] == rows) & (rows < capacity) & (
        chosen[None, :] == 1
    )
    row_weight = jnp.sum(jnp.where(dispatch, weight[None, :], 0.0), axis=1)
    dispatch = dispatch.astype(jnp.bfloat16)

    tokens = spread(lines, "seq", plane, flat).reshape(q_tok, quarter * width)
    routed = dot(dispatch[:gain_row], tokens).astype(jnp.bfloat16)
    spare = jnp.zeros((rows.shape[0] - gain_row - 1, quarter * width), jnp.bfloat16)
    mine = jnp.concatenate([routed, gain, spare])
    other = swap(mine, "exp", 1)
    kept, sent = feed(gain_row, core[None], mine, other, w_gate, w_up, w_down)

    half = kept + swap(sent, "exp", 1).astype(jnp.float32)
    half = (half * row_weight[:, None]).astype(jnp.bfloat16)
    rows = jnp.dot(dispatch.T, half, preferred_element_type=jnp.float32).astype(jnp.bfloat16)
    rows = exchange(rows.reshape(plane, run, quarter * group, HD), "seq", flat)
    rows = jnp.sum(rows.astype(jnp.float32), axis=0).astype(jnp.bfloat16)
    rows = exchange(rows.reshape(run * quarter, group, HD), ("seq", "exp"), tall)
    expert_rows = jnp.sum(rows.astype(jnp.float32), axis=0)
    return (attention.astype(jnp.float32) + expert_rows).astype(jnp.bfloat16).reshape(1, width)


def solution(mesh):
    in_specs = (
        P("seq", "exp"),
        P("seq", "exp"),
        P("seq", "exp"),
        P("seq", "exp"),
        P("seq", "exp"),
        P(),
        P("exp"),
        P(),
        P(),
        P(None, ("seq", "exp")),
        P(None, ("seq", "exp")),
        P(("seq", "exp"), None),
    )
    out_specs = P("seq", "exp")
    return jax.shard_map(local, mesh=mesh, in_specs=in_specs, out_specs=out_specs, check_vma=False)
```

```python
import functools

import jax
import jax.numpy as jnp
from jax import lax
from jax.experimental import pallas as pl
from jax.experimental.pallas import tpu as pltpu
from jax.sharding import PartitionSpec as P

D = 6144
HEADS = 48
KV_HEADS = 8
HD = 128
FF = 16384


ROPE_BASE = 1000000.0
NORM_EPS = 1e-05
MASKED = -1e30


def frequencies(width):
    index = jnp.arange(width // 2, dtype=jnp.float32)
    return ROPE_BASE ** (-2.0 * index / width)


def rotate(values, angles):
    half = values.shape[-1] // 2
    first = values[..., :half]
    second = values[..., half:]
    cosine = jnp.cos(angles)
    sine = jnp.sin(angles)
    return jnp.concatenate(
        [first * cosine - second * sine, second * cosine + first * sine], axis=-1
    )


def dot(left, right):
    return jnp.dot(left, right, preferred_element_type=jnp.float32)


def dot_rows(left, right):
    return lax.dot_general(
        left, right, (((1,), (1,)), ((), ())), preferred_element_type=jnp.float32
    )


def copies_kernel(row_ref, out_ref):
    group = out_ref.shape[1]
    row = row_ref[...].astype(jnp.float32)
    block = jnp.concatenate([row[:, h * HD : (h + 1) * HD] for h in range(group)], 0)
    out_ref[...] = jnp.broadcast_to(block[None], out_ref.shape).astype(out_ref.dtype)


def row_copies(row, count, group):
    return pl.pallas_call(
        copies_kernel,
        out_shape=jax.ShapeDtypeStruct((count, group, HD), row.dtype),
    )(row)


def attend_kernel(
    context,
    place_ref,
    near_ref,
    far_ref,
    rotated_ref,
    keys_ref,
    values_ref,
    fresh_rotated_ref,
    fresh_key_ref,
    fresh_value_ref,
    out_ref,
    wide_ref,
):
    q_tok = out_ref.shape[0]
    rows, ctx_dev = near_ref.shape[0], keys_ref.shape[0]
    group = rows // q_tok
    scale = HD ** (-0.5)
    start, limit, seq_at = place_ref[0], place_ref[1], place_ref[2]
    near_query = near_ref[...]
    far_query = far_ref[...]
    token = lax.broadcasted_iota(jnp.int32, (rows, ctx_dev), 0) & (q_tok - 1)
    key_pos = start + lax.broadcasted_iota(jnp.int32, (rows, ctx_dev), 1)
    distance = context + token - key_pos
    near = dot_rows(near_query, rotated_ref[...])
    far = dot_rows(far_query, keys_ref[...])
    score = jnp.where(distance < limit, near, far) * scale
    distance = (lax.broadcasted_iota(jnp.int32, (rows, 1), 0) & (q_tok - 1)) - seq_at
    fresh_rotated = fresh_rotated_ref[...].astype(jnp.float32)
    fresh_key = fresh_key_ref[...].astype(jnp.float32)
    near = jnp.sum(near_query.astype(jnp.float32) * fresh_rotated, axis=1, keepdims=True)
    far = jnp.sum(far_query.astype(jnp.float32) * fresh_key, axis=1, keepdims=True)
    fresh = jnp.where(distance < limit, near, far) * scale
    fresh = jnp.where(distance >= 0, fresh, MASKED)
    high = jnp.maximum(jnp.max(score, axis=1, keepdims=True), fresh)
    high = high.astype(jnp.bfloat16).astype(jnp.float32)
    expo = jnp.exp(score - high)
    fresh = jnp.exp(fresh - high)
    total = jnp.sum(expo, axis=1, keepdims=True) + fresh
    sums = dot(expo.astype(jnp.bfloat16), values_ref[...])
    fresh = fresh.astype(jnp.bfloat16).astype(jnp.float32)
    sums = sums + fresh * fresh_value_ref[...].astype(jnp.float32)
    total_high = total.astype(jnp.bfloat16).astype(jnp.float32)
    total_low = total - total_high
    lane = lax.broadcasted_iota(jnp.int32, (q_tok, HD), 1)
    facts = jnp.zeros((q_tok, HD), jnp.float32)
    for h in range(group):
        part = slice(h * q_tok, (h + 1) * q_tok)
        wide_ref[:, h, :] = sums[part]
        facts = jnp.where(lane == h, high[part], facts)
        facts = jnp.where(lane == group + h, total_high[part], facts)
        facts = jnp.where(lane == 2 * group + h, total_low[part], facts)
    wide_ref[:, group, :] = facts
    wide_ref[:, group + 1, :] = jnp.zeros((q_tok, HD), jnp.float32)
    out_ref[...] = wide_ref[...].astype(out_ref.dtype)


def attend(context, q_tok, place, *arrays):
    rows = arrays[0].shape[0] // q_tok + 2
    vmem = pl.BlockSpec(memory_space=pltpu.VMEM)
    return pl.pallas_call(
        functools.partial(attend_kernel, context),
        out_shape=jax.ShapeDtypeStruct((q_tok, rows, HD), jnp.bfloat16),
        in_specs=[pl.BlockSpec(memory_space=pltpu.SMEM)] + [vmem] * len(arrays),
        out_specs=vmem,
        scratch_shapes=[pltpu.VMEM((q_tok, rows, HD), jnp.float32)],
        compiler_params=pltpu.CompilerParams(vmem_limit_bytes=16 << 20),
    )(place, *arrays)


def expert_kernel(
    gain_row,
    place_ref,
    mine_ref,
    other_ref,
    w_gate,
    w_up,
    w_down,
    kept_ref,
    sent_ref,
    gate_ref,
    up_ref,
    down_ref,
    sems,
):
    rows, half = mine_ref.shape
    depth = w_gate.shape[0]
    steps = 4
    width = half // steps
    core = place_ref[0]
    copies = []
    for i in range(steps):
        part = pl.ds(i * (depth // steps), depth // steps)
        for j, (source, target) in enumerate(((w_gate, gate_ref), (w_up, up_ref))):
            copy = pltpu.make_async_copy(source.at[part], target.at[part], sems.at[2 * i + j])
            copy.start()
            copies.append(copy)
    last = pltpu.make_async_copy(w_down, down_ref, sems.at[2 * steps])
    last.start()

    mine = mine_ref[...].astype(jnp.float32)
    other = other_ref[...].astype(jnp.float32)
    squares = jnp.sum(mine * mine, axis=1, keepdims=True)
    squares = squares + jnp.sum(other * other, axis=1, keepdims=True)
    scale = lax.rsqrt(squares / D + NORM_EPS)
    mine = (mine * scale * mine[gain_row : gain_row + 1]).astype(jnp.bfloat16)
    other = (other * scale * other[gain_row : gain_row + 1]).astype(jnp.bfloat16)
    gate = jnp.zeros((rows, gate_ref.shape[1]), jnp.float32)
    upward = gate
    for i in range(steps):
        copies[2 * i].wait()
        copies[2 * i + 1].wait()
        for side, values in ((core, mine), (1 - core, other)):
            part = pl.ds(pl.multiple_of((2 * i + side) * width, width), width)
            block = values[:, i * width : (i + 1) * width]
            gate = gate + dot(block, gate_ref[part, :])
            upward = upward + dot(block, up_ref[part, :])
    hidden = (gate / (1.0 + jnp.exp(-gate)) * upward).astype(jnp.bfloat16)
    last.wait()
    for i in range(steps):
        part = pl.ds(pl.multiple_of((2 * i + 1 - core) * width, width), width)
        columns = slice(i * width, (i + 1) * width)
        sent_ref[:, columns] = dot(hidden, down_ref[:, part]).astype(sent_ref.dtype)
        part = pl.ds(pl.multiple_of((2 * i + core) * width, width), width)
        kept_ref[:, columns] = dot(hidden, down_ref[:, part])


def feed(gain_row, place, mine, other, w_gate, w_up, w_down):
    vmem = pl.BlockSpec(memory_space=pltpu.VMEM)
    far_memory = pl.BlockSpec(memory_space=pltpu.HBM)
    return pl.pallas_call(
        functools.partial(expert_kernel, gain_row),
        out_shape=(
            jax.ShapeDtypeStruct(mine.shape, jnp.float32),
            jax.ShapeDtypeStruct(mine.shape, jnp.bfloat16),
        ),
        in_specs=[pl.BlockSpec(memory_space=pltpu.SMEM), vmem, vmem] + [far_memory] * 3,
        out_specs=(vmem, vmem),
        scratch_shapes=[
            pltpu.VMEM(w_gate.shape, w_gate.dtype),
            pltpu.VMEM(w_up.shape, w_up.dtype),
            pltpu.VMEM(w_down.shape, w_down.dtype),
            pltpu.SemaphoreType.DMA((9,)),
        ],
        compiler_params=pltpu.CompilerParams(vmem_limit_bytes=52 << 20),
    )(place, mine, other, w_gate, w_up, w_down)


def swap(value, axis, mask):
    size = lax.axis_size(axis)
    return lax.ppermute(value, axis, [(i, i ^ mask) for i in range(size)])


def exchange(value, axis, groups=None):
    return lax.all_to_all(value, axis, 0, 0, axis_index_groups=groups, tiled=True)


def spread(value, axis, count, groups=None):
    return exchange(jnp.broadcast_to(value[None], (count, *value.shape)), axis, groups)


def local(
    queries,
    key_cache,
    value_cache,
    key_new,
    value_new,
    window,
    norm_gain,
    expert_ids,
    gate_values,
    w_gate,
    w_up,
    w_down,
):
    seq_count = lax.axis_size("seq")
    exp_count = lax.axis_size("exp")
    seq_at = lax.axis_index("seq")
    exp_at = lax.axis_index("exp")
    group = HEADS // KV_HEADS
    width = group * HD
    ctx_dev = key_cache.shape[0]
    q_tok = seq_count
    context = ctx_dev * seq_count
    freq = frequencies(HD)
    limit = window[0]
    quarter = exp_count // 2
    core = exp_at % 2
    run = seq_count // 16
    plane = seq_count // run
    flat = [[run * i + j for i in range(plane)] for j in range(run)]
    tall = [
        [(run * i + j) * exp_count + 2 * h + c for j in range(run) for h in range(quarter)]
        for i in range(plane)
        for c in range(2)
    ]

    stretch = exchange(row_copies(queries, seq_count, group), "seq")
    stretch, expert_ids, gate_values = lax.optimization_barrier(
        (stretch, expert_ids, gate_values)
    )
    query_pos = context + jnp.arange(q_tok, dtype=jnp.int32)
    query_f32 = stretch.astype(jnp.float32)
    near_query = rotate(
        query_f32, query_pos.astype(jnp.float32)[:, None, None] * freq
    ).astype(jnp.bfloat16)
    far_query = rotate(query_f32, limit.astype(jnp.float32) * freq).astype(jnp.bfloat16)
    near_query = jnp.transpose(near_query, (1, 0, 2)).reshape(group * q_tok, HD)
    far_query = jnp.transpose(far_query, (1, 0, 2)).reshape(group * q_tok, HD)
    key_pos = seq_at * ctx_dev + jnp.arange(ctx_dev, dtype=jnp.int32)
    rotated_cache = rotate(
        key_cache.astype(jnp.float32), key_pos.astype(jnp.float32)[:, None] * freq
    ).astype(jnp.bfloat16)
    rotated_fresh = rotate(
        key_new.astype(jnp.float32), (context + seq_at).astype(jnp.float32) * freq
    ).astype(jnp.bfloat16)
    place = jnp.stack([seq_at * ctx_dev, limit, seq_at])
    parts = attend(
        context,
        q_tok,
        place,
        near_query,
        far_query,
        rotated_cache,
        key_cache,
        value_cache,
        rotated_fresh,
        key_new,
        value_new,
    )

    parts = exchange(parts.reshape(plane, run, group + 2, HD), "seq", flat)
    parts = parts.astype(jnp.float32)
    maxima = parts[:, :, group, :group]
    totals = parts[:, :, group, group : 2 * group] + parts[:, :, group, 2 * group : 3 * group]
    top = jnp.max(maxima, axis=0)
    weights = jnp.exp(maxima - top)
    total = jnp.sum(weights * totals, axis=0)
    sums = jnp.sum(weights[..., None] * parts[:, :, :group, :], axis=0).astype(jnp.bfloat16)
    total_high = total.astype(jnp.bfloat16)
    total_low = (total - total_high.astype(jnp.float32)).astype(jnp.bfloat16)
    facts = jnp.concatenate(
        [top.astype(jnp.bfloat16).ravel(), total_high.ravel(), total_low.ravel()]
    )
    facts = jnp.pad(facts, (0, HD - facts.shape[0]))[None]
    lines = jnp.concatenate(
        [
            sums.reshape(run * group, HD),
            facts,
            norm_gain.reshape(group, HD),
            jnp.zeros((1, HD), jnp.bfloat16),
        ]
    )
    lines = spread(lines, ("seq", "exp"), run * quarter, tall)
    lines = lines.reshape(run, quarter, -1, HD)
    gain = lines[0, :, run * group + 1 : run * group + 1 + group]
    facts = lines[:, :, run * group, : 3 * run * group].astype(jnp.float32)
    facts = facts.reshape(run, quarter, 3, run, group)
    weights = jnp.exp(facts[:, :, 0] - jnp.max(facts[:, :, 0], axis=0))
    below = jnp.sum(weights * (facts[:, :, 1] + facts[:, :, 2]), axis=0)
    sums = lines[:, :, : run * group].astype(jnp.float32).reshape(run, quarter, run, group, HD)
    above = jnp.sum(weights[..., None] * sums, axis=0)
    attention = (above / below[..., None]).astype(jnp.bfloat16)
    attention = jnp.transpose(attention, (1, 0, 2, 3))

    ff_dev = w_gate.shape[1]
    expert = (seq_at * exp_count + exp_at) * ff_dev // FF
    capacity = (q_tok * 17 + 31) // 32
    matched = (expert_ids == expert).astype(jnp.int32)
    chosen = jnp.sum(matched, axis=1)
    weight = jnp.sum(gate_values * matched.astype(jnp.float32), axis=1)
    slot = jnp.cumsum(chosen) - chosen
    gain_row = -(-capacity // 8) * 8
    rows = jnp.arange(-(-(gain_row + 1) // 16) * 16, dtype=jnp.int32)[:, None]
    dispatch = (slot[None, :] == rows) & (rows < capacity) & (
        chosen[None, :] == 1
    )
    row_weight = jnp.sum(jnp.where(dispatch, weight[None, :], 0.0), axis=1)
    dispatch = dispatch.astype(jnp.bfloat16)

    tokens = spread(attention.reshape(run, quarter * group, HD), "seq", plane, flat)
    tokens = tokens.reshape(q_tok, quarter * width)
    routed = dot(dispatch[:gain_row], tokens).astype(jnp.bfloat16)
    spare = jnp.zeros((rows.shape[0] - gain_row - 1, quarter * width), jnp.bfloat16)
    mine = jnp.concatenate([routed, gain.reshape(1, -1), spare])
    other = swap(mine, "exp", 1)
    kept, sent = feed(gain_row, core[None], mine, other, w_gate, w_up, w_down)

    half = kept + swap(sent, "exp", 1).astype(jnp.float32)
    half = (half * row_weight[:, None]).astype(jnp.bfloat16)
    rows = jnp.dot(dispatch.T, half, preferred_element_type=jnp.float32).astype(jnp.bfloat16)
    rows = exchange(rows.reshape(plane, run, quarter * group, HD), "seq", flat)
    rows = jnp.sum(rows.astype(jnp.float32), axis=0).astype(jnp.bfloat16)
    rows = exchange(rows.reshape(run * quarter, group, HD), ("seq", "exp"), tall)
    expert_rows = jnp.sum(rows.astype(jnp.float32), axis=0)
    own = attention.reshape(run * quarter, group, HD)
    own = lax.dynamic_index_in_dim(own, seq_at % run * quarter + exp_at // 2, 0, False)
    return (own.astype(jnp.float32) + expert_rows).astype(jnp.bfloat16).reshape(1, width)


def solution(mesh):
    in_specs = (
        P("seq", "exp"),
        P("seq", "exp"),
        P("seq", "exp"),
        P("seq", "exp"),
        P("seq", "exp"),
        P(),
        P("exp"),
        P(),
        P(),
        P(None, ("seq", "exp")),
        P(None, ("seq", "exp")),
        P(("seq", "exp"), None),
    )
    out_specs = P("seq", "exp")
    return jax.shard_map(local, mesh=mesh, in_specs=in_specs, out_specs=out_specs, check_vma=False)
```

```python
import functools

import jax
import jax.numpy as jnp
from jax import lax
from jax.experimental import pallas as pl
from jax.experimental.pallas import tpu as pltpu
from jax.sharding import PartitionSpec as P

D = 6144
HEADS = 48
KV_HEADS = 8
HD = 128
FF = 16384


ROPE_BASE = 1000000.0
NORM_EPS = 1e-05
MASKED = -1e30


def frequencies(width):
    index = jnp.arange(width // 2, dtype=jnp.float32)
    return ROPE_BASE ** (-2.0 * index / width)


def rotate(values, angles):
    half = values.shape[-1] // 2
    first = values[..., :half]
    second = values[..., half:]
    cosine = jnp.cos(angles)
    sine = jnp.sin(angles)
    return jnp.concatenate(
        [first * cosine - second * sine, second * cosine + first * sine], axis=-1
    )


def dot(left, right):
    return jnp.dot(left, right, preferred_element_type=jnp.float32)


def dot_rows(left, right):
    return lax.dot_general(
        left, right, (((1,), (1,)), ((), ())), preferred_element_type=jnp.float32
    )


def copies_kernel(row_ref, out_ref):
    group = out_ref.shape[1]
    row = row_ref[...].astype(jnp.float32)
    block = jnp.concatenate([row[:, h * HD : (h + 1) * HD] for h in range(group)], 0)
    out_ref[...] = jnp.broadcast_to(block[None], out_ref.shape).astype(out_ref.dtype)


def row_copies(row, count, group):
    return pl.pallas_call(
        copies_kernel,
        out_shape=jax.ShapeDtypeStruct((count, group, HD), row.dtype),
    )(row)


def attend_kernel(
    context,
    place_ref,
    near_ref,
    far_ref,
    rotated_ref,
    keys_ref,
    values_ref,
    fresh_rotated_ref,
    fresh_key_ref,
    fresh_value_ref,
    out_ref,
    wide_ref,
):
    q_tok = out_ref.shape[0]
    rows, ctx_dev = near_ref.shape[0], keys_ref.shape[0]
    group = rows // q_tok
    scale = HD ** (-0.5)
    start, limit, seq_at = place_ref[0], place_ref[1], place_ref[2]
    near_query = near_ref[...]
    far_query = far_ref[...]
    token = lax.broadcasted_iota(jnp.int32, (rows, ctx_dev), 0) & (q_tok - 1)
    key_pos = start + lax.broadcasted_iota(jnp.int32, (rows, ctx_dev), 1)
    distance = context + token - key_pos
    near = dot_rows(near_query, rotated_ref[...])
    far = dot_rows(far_query, keys_ref[...])
    score = jnp.where(distance < limit, near, far) * scale
    distance = (lax.broadcasted_iota(jnp.int32, (rows, 1), 0) & (q_tok - 1)) - seq_at
    fresh_rotated = fresh_rotated_ref[...].astype(jnp.float32)
    fresh_key = fresh_key_ref[...].astype(jnp.float32)
    near = jnp.sum(near_query.astype(jnp.float32) * fresh_rotated, axis=1, keepdims=True)
    far = jnp.sum(far_query.astype(jnp.float32) * fresh_key, axis=1, keepdims=True)
    fresh = jnp.where(distance < limit, near, far) * scale
    fresh = jnp.where(distance >= 0, fresh, MASKED)
    high = jnp.maximum(jnp.max(score, axis=1, keepdims=True), fresh)
    high = high.astype(jnp.bfloat16).astype(jnp.float32)
    expo = jnp.exp(score - high)
    fresh = jnp.exp(fresh - high)
    total = jnp.sum(expo, axis=1, keepdims=True) + fresh
    sums = dot(expo.astype(jnp.bfloat16), values_ref[...])
    fresh = fresh.astype(jnp.bfloat16).astype(jnp.float32)
    sums = sums + fresh * fresh_value_ref[...].astype(jnp.float32)
    total_high = total.astype(jnp.bfloat16).astype(jnp.float32)
    total_low = total - total_high
    lane = lax.broadcasted_iota(jnp.int32, (q_tok, HD), 1)
    facts = jnp.zeros((q_tok, HD), jnp.float32)
    for h in range(group):
        part = slice(h * q_tok, (h + 1) * q_tok)
        wide_ref[:, h, :] = sums[part]
        facts = jnp.where(lane == h, high[part], facts)
        facts = jnp.where(lane == group + h, total_high[part], facts)
        facts = jnp.where(lane == 2 * group + h, total_low[part], facts)
    wide_ref[:, group, :] = facts
    wide_ref[:, group + 1, :] = jnp.zeros((q_tok, HD), jnp.float32)
    out_ref[...] = wide_ref[...].astype(out_ref.dtype)


def attend(context, q_tok, place, *arrays):
    rows = arrays[0].shape[0] // q_tok + 2
    vmem = pl.BlockSpec(memory_space=pltpu.VMEM)
    return pl.pallas_call(
        functools.partial(attend_kernel, context),
        out_shape=jax.ShapeDtypeStruct((q_tok, rows, HD), jnp.bfloat16),
        in_specs=[pl.BlockSpec(memory_space=pltpu.SMEM)] + [vmem] * len(arrays),
        out_specs=vmem,
        scratch_shapes=[pltpu.VMEM((q_tok, rows, HD), jnp.float32)],
        compiler_params=pltpu.CompilerParams(vmem_limit_bytes=16 << 20),
    )(place, *arrays)


def head_columns(tiles, group):
    row = tiles[..., group : group + 1, :]
    shape = tiles.shape[-2:]
    lane = lax.broadcasted_iota(jnp.int32, shape, 1)
    head = lax.broadcasted_iota(jnp.int32, shape, 0)
    columns = [
        jnp.sum(jnp.where((lane == head + i * group) & (head < group), row, 0.0), -1, keepdims=True)
        for i in range(3)
    ]
    return columns[0], columns[1] + columns[2]


def merged(tiles, group):
    maxima, totals = head_columns(tiles, group)
    high = jnp.max(maxima, axis=0)
    weights = jnp.exp(maxima - high)
    return high, jnp.sum(weights * totals, axis=0), jnp.sum(weights * tiles, axis=0)


def copy_to_all(block_ref, out_ref, sems):
    copies = [
        pltpu.make_async_copy(block_ref, out_ref.at[i], sems.at[i])
        for i in range(out_ref.shape[0])
    ]
    for copy in copies:
        copy.start()
    for copy in copies:
        copy.wait()


def first_merge_kernel(parts_ref, gain_ref, out_ref, block_ref, sems):
    run, tile = parts_ref.shape[1:3]
    group = gain_ref.shape[0]
    high, total, sums = merged(parts_ref[...].astype(jnp.float32), group)
    total_high = total.astype(jnp.bfloat16).astype(jnp.float32)
    total_low = total - total_high
    lane = lax.broadcasted_iota(jnp.int32, (tile, HD), 1)
    head = lax.broadcasted_iota(jnp.int32, (tile, HD), 0)
    facts = jnp.zeros_like(sums)
    for i, column in enumerate((high, total_high, total_low)):
        facts = jnp.where((lane == head + i * group) & (head < group), column, facts)
    facts = jnp.sum(facts, axis=1, keepdims=True)
    sums = jnp.where(head < group, sums, jnp.where(head == group, facts, 0.0))
    block_ref[:run] = sums.astype(block_ref.dtype)
    gain = gain_ref[...].astype(jnp.float32)
    gain = jnp.concatenate([gain, jnp.zeros((tile - group, HD), jnp.float32)])
    block_ref[run] = gain.astype(block_ref.dtype)
    copy_to_all(block_ref, out_ref, sems)


def first_merge(parts, gain, copies):
    run, tile, width = parts.shape[1:]
    return pl.pallas_call(
        first_merge_kernel,
        out_shape=jax.ShapeDtypeStruct((copies, run + 1, tile, width), jnp.bfloat16),
        in_specs=[pl.BlockSpec(memory_space=pltpu.VMEM)] * 2,
        out_specs=pl.BlockSpec(memory_space=pl.ANY),
        scratch_shapes=[
            pltpu.VMEM((run + 1, tile, width), jnp.bfloat16),
            pltpu.SemaphoreType.DMA((copies,)),
        ],
    )(parts, gain)


def last_merge_kernel(group, lines_ref, out_ref, wide_ref, block_ref, sems):
    run, rows = block_ref.shape[:2]
    quarter = rows // group
    tile = lines_ref.shape[2]
    lines = lines_ref[...].astype(jnp.float32)[:, :run]
    lines = lines.reshape(lines.shape[0] // quarter, quarter * run, tile, HD)
    high, total, sums = merged(lines, group)
    head = lax.broadcasted_iota(jnp.int32, total.shape, 1)
    heads = sums / jnp.where(head < group, total, 1.0)
    for h in range(quarter):
        for t in range(run):
            wide_ref[t, h * group : (h + 1) * group, :] = heads[h * run + t, :group]
    block_ref[...] = wide_ref[...].astype(block_ref.dtype)
    copy_to_all(block_ref, out_ref, sems)


def last_merge(lines, group, quarter, copies):
    run = lines.shape[1] - 1
    block = (run, quarter * group, HD)
    return pl.pallas_call(
        functools.partial(last_merge_kernel, group),
        out_shape=jax.ShapeDtypeStruct((copies, *block), jnp.bfloat16),
        in_specs=[pl.BlockSpec(memory_space=pltpu.VMEM)],
        out_specs=pl.BlockSpec(memory_space=pl.ANY),
        scratch_shapes=[
            pltpu.VMEM(block, jnp.float32),
            pltpu.VMEM(block, jnp.bfloat16),
            pltpu.SemaphoreType.DMA((copies,)),
        ],
    )(lines)


def expert_kernel(
    gain_row,
    place_ref,
    mine_ref,
    other_ref,
    w_gate,
    w_up,
    w_down,
    kept_ref,
    sent_ref,
    gate_ref,
    up_ref,
    down_ref,
    sems,
):
    rows, half = mine_ref.shape
    depth = w_gate.shape[0]
    steps = 4
    width = half // steps
    core = place_ref[0]
    copies = []
    for i in range(steps):
        part = pl.ds(i * (depth // steps), depth // steps)
        for j, (source, target) in enumerate(((w_gate, gate_ref), (w_up, up_ref))):
            copy = pltpu.make_async_copy(source.at[part], target.at[part], sems.at[2 * i + j])
            copy.start()
            copies.append(copy)
    last = pltpu.make_async_copy(w_down, down_ref, sems.at[2 * steps])
    last.start()

    mine = mine_ref[...].astype(jnp.float32)
    other = other_ref[...].astype(jnp.float32)
    squares = jnp.sum(mine * mine, axis=1, keepdims=True)
    squares = squares + jnp.sum(other * other, axis=1, keepdims=True)
    scale = lax.rsqrt(squares / D + NORM_EPS)
    mine = (mine * scale * mine[gain_row : gain_row + 1]).astype(jnp.bfloat16)
    other = (other * scale * other[gain_row : gain_row + 1]).astype(jnp.bfloat16)
    gate = jnp.zeros((rows, gate_ref.shape[1]), jnp.float32)
    upward = gate
    for i in range(steps):
        copies[2 * i].wait()
        copies[2 * i + 1].wait()
        for side, values in ((core, mine), (1 - core, other)):
            part = pl.ds(pl.multiple_of((2 * i + side) * width, width), width)
            block = values[:, i * width : (i + 1) * width]
            gate = gate + dot(block, gate_ref[part, :])
            upward = upward + dot(block, up_ref[part, :])
    hidden = (gate / (1.0 + jnp.exp(-gate)) * upward).astype(jnp.bfloat16)
    last.wait()
    for i in range(steps):
        part = pl.ds(pl.multiple_of((2 * i + 1 - core) * width, width), width)
        columns = slice(i * width, (i + 1) * width)
        sent_ref[:, columns] = dot(hidden, down_ref[:, part]).astype(sent_ref.dtype)
        part = pl.ds(pl.multiple_of((2 * i + core) * width, width), width)
        kept_ref[:, columns] = dot(hidden, down_ref[:, part])


def feed(gain_row, place, mine, other, w_gate, w_up, w_down):
    vmem = pl.BlockSpec(memory_space=pltpu.VMEM)
    far_memory = pl.BlockSpec(memory_space=pltpu.HBM)
    return pl.pallas_call(
        functools.partial(expert_kernel, gain_row),
        out_shape=(
            jax.ShapeDtypeStruct(mine.shape, jnp.float32),
            jax.ShapeDtypeStruct(mine.shape, jnp.bfloat16),
        ),
        in_specs=[pl.BlockSpec(memory_space=pltpu.SMEM), vmem, vmem] + [far_memory] * 3,
        out_specs=(vmem, vmem),
        scratch_shapes=[
            pltpu.VMEM(w_gate.shape, w_gate.dtype),
            pltpu.VMEM(w_up.shape, w_up.dtype),
            pltpu.VMEM(w_down.shape, w_down.dtype),
            pltpu.SemaphoreType.DMA((9,)),
        ],
        compiler_params=pltpu.CompilerParams(vmem_limit_bytes=52 << 20),
    )(place, mine, other, w_gate, w_up, w_down)


def swap(value, axis, mask):
    size = lax.axis_size(axis)
    return lax.ppermute(value, axis, [(i, i ^ mask) for i in range(size)])


def exchange(value, axis, groups=None):
    return lax.all_to_all(value, axis, 0, 0, axis_index_groups=groups, tiled=True)


def spread(value, axis, count, groups=None):
    return exchange(jnp.broadcast_to(value[None], (count, *value.shape)), axis, groups)


def local(
    queries,
    key_cache,
    value_cache,
    key_new,
    value_new,
    window,
    norm_gain,
    expert_ids,
    gate_values,
    w_gate,
    w_up,
    w_down,
):
    seq_count = lax.axis_size("seq")
    exp_count = lax.axis_size("exp")
    seq_at = lax.axis_index("seq")
    exp_at = lax.axis_index("exp")
    group = HEADS // KV_HEADS
    width = group * HD
    ctx_dev = key_cache.shape[0]
    q_tok = seq_count
    context = ctx_dev * seq_count
    freq = frequencies(HD)
    limit = window[0]
    quarter = exp_count // 2
    core = exp_at % 2
    run = seq_count // 16
    plane = seq_count // run
    flat = [[run * i + j for i in range(plane)] for j in range(run)]
    tall = [
        [(run * i + j) * exp_count + 2 * h + c for j in range(run) for h in range(quarter)]
        for i in range(plane)
        for c in range(2)
    ]

    stretch = exchange(row_copies(queries, seq_count, group), "seq")
    stretch, expert_ids, gate_values = lax.optimization_barrier(
        (stretch, expert_ids, gate_values)
    )
    query_pos = context + jnp.arange(q_tok, dtype=jnp.int32)
    query_f32 = stretch.astype(jnp.float32)
    near_query = rotate(
        query_f32, query_pos.astype(jnp.float32)[:, None, None] * freq
    ).astype(jnp.bfloat16)
    far_query = rotate(query_f32, limit.astype(jnp.float32) * freq).astype(jnp.bfloat16)
    near_query = jnp.transpose(near_query, (1, 0, 2)).reshape(group * q_tok, HD)
    far_query = jnp.transpose(far_query, (1, 0, 2)).reshape(group * q_tok, HD)
    key_pos = seq_at * ctx_dev + jnp.arange(ctx_dev, dtype=jnp.int32)
    rotated_cache = rotate(
        key_cache.astype(jnp.float32), key_pos.astype(jnp.float32)[:, None] * freq
    ).astype(jnp.bfloat16)
    rotated_fresh = rotate(
        key_new.astype(jnp.float32), (context + seq_at).astype(jnp.float32) * freq
    ).astype(jnp.bfloat16)
    place = jnp.stack([seq_at * ctx_dev, limit, seq_at])
    parts = attend(
        context,
        q_tok,
        place,
        near_query,
        far_query,
        rotated_cache,
        key_cache,
        value_cache,
        rotated_fresh,
        key_new,
        value_new,
    )

    parts = exchange(parts.reshape(plane, run, group + 2, HD), "seq", flat)
    lines = first_merge(parts, norm_gain.reshape(group, HD), run * quarter)
    lines = exchange(lines, ("seq", "exp"), tall)
    gain = lines[:quarter, run, :group].reshape(1, quarter * width)
    tokens = last_merge(lines, group, quarter, plane)
    attention = tokens[0]

    ff_dev = w_gate.shape[1]
    expert = (seq_at * exp_count + exp_at) * ff_dev // FF
    capacity = (q_tok * 17 + 31) // 32
    matched = (expert_ids == expert).astype(jnp.int32)
    chosen = jnp.sum(matched, axis=1)
    weight = jnp.sum(gate_values * matched.astype(jnp.float32), axis=1)
    slot = jnp.cumsum(chosen) - chosen
    gain_row = -(-capacity // 8) * 8
    rows = jnp.arange(-(-(gain_row + 1) // 16) * 16, dtype=jnp.int32)[:, None]
    dispatch = (slot[None, :] == rows) & (rows < capacity) & (
        chosen[None, :] == 1
    )
    row_weight = jnp.sum(jnp.where(dispatch, weight[None, :], 0.0), axis=1)
    dispatch = dispatch.astype(jnp.bfloat16)

    tokens = exchange(tokens, "seq", flat).reshape(q_tok, quarter * width)
    routed = dot(dispatch[:gain_row], tokens).astype(jnp.bfloat16)
    spare = jnp.zeros((rows.shape[0] - gain_row - 1, quarter * width), jnp.bfloat16)
    mine = jnp.concatenate([routed, gain, spare])
    other = swap(mine, "exp", 1)
    kept, sent = feed(gain_row, core[None], mine, other, w_gate, w_up, w_down)

    half = kept + swap(sent, "exp", 1).astype(jnp.float32)
    half = (half * row_weight[:, None]).astype(jnp.bfloat16)
    rows = jnp.dot(dispatch.T, half, preferred_element_type=jnp.float32).astype(jnp.bfloat16)
    rows = exchange(rows.reshape(plane, run, quarter * group, HD), "seq", flat)
    rows = jnp.sum(rows.astype(jnp.float32), axis=0).astype(jnp.bfloat16)
    rows = exchange(rows.reshape(run * quarter, group, HD), ("seq", "exp"), tall)
    expert_rows = jnp.sum(rows.astype(jnp.float32), axis=0)
    own = lax.dynamic_index_in_dim(attention, seq_at % run, 0, False)
    own = lax.dynamic_slice_in_dim(own, exp_at // 2 * group, group, 0)
    return (own.astype(jnp.float32) + expert_rows).astype(jnp.bfloat16).reshape(1, width)


def solution(mesh):
    in_specs = (
        P("seq", "exp"),
        P("seq", "exp"),
        P("seq", "exp"),
        P("seq", "exp"),
        P("seq", "exp"),
        P(),
        P("exp"),
        P(),
        P(),
        P(None, ("seq", "exp")),
        P(None, ("seq", "exp")),
        P(("seq", "exp"), None),
    )
    out_specs = P("seq", "exp")
    return jax.shard_map(local, mesh=mesh, in_specs=in_specs, out_specs=out_specs, check_vma=False)
```

```python
import functools

import jax
import jax.numpy as jnp
from jax import lax
from jax.experimental import pallas as pl
from jax.experimental.pallas import tpu as pltpu
from jax.sharding import PartitionSpec as P

D = 6144
HEADS = 48
KV_HEADS = 8
HD = 128
FF = 16384


ROPE_BASE = 1000000.0
NORM_EPS = 1e-05
MASKED = -1e30


def frequencies(width):
    index = jnp.arange(width // 2, dtype=jnp.float32)
    return ROPE_BASE ** (-2.0 * index / width)


def rotate(values, angles):
    half = values.shape[-1] // 2
    first = values[..., :half]
    second = values[..., half:]
    cosine = jnp.cos(angles)
    sine = jnp.sin(angles)
    return jnp.concatenate(
        [first * cosine - second * sine, second * cosine + first * sine], axis=-1
    )


def dot(left, right):
    return jnp.dot(left, right, preferred_element_type=jnp.float32)


def dot_rows(left, right):
    return lax.dot_general(
        left, right, (((1,), (1,)), ((), ())), preferred_element_type=jnp.float32
    )


def copies_kernel(row_ref, out_ref):
    group = out_ref.shape[1]
    row = row_ref[...].astype(jnp.float32)
    block = jnp.concatenate([row[:, h * HD : (h + 1) * HD] for h in range(group)], 0)
    out_ref[...] = jnp.broadcast_to(block[None], out_ref.shape).astype(out_ref.dtype)


def row_copies(row, count, group):
    return pl.pallas_call(
        copies_kernel,
        out_shape=jax.ShapeDtypeStruct((count, group, HD), row.dtype),
    )(row)


def attend_kernel(
    context,
    place_ref,
    near_ref,
    far_ref,
    rotated_ref,
    keys_ref,
    values_ref,
    fresh_rotated_ref,
    fresh_key_ref,
    fresh_value_ref,
    dispatch_ref,
    weight_ref,
    out_ref,
    later_ref,
    dispatch_out_ref,
    weight_out_ref,
    wide_ref,
):
    later_ref[0] = place_ref[3]
    later_ref[1] = place_ref[4]
    dispatch_out_ref[...] = dispatch_ref[...]
    weight_out_ref[...] = weight_ref[...]
    q_tok = out_ref.shape[0]
    rows, ctx_dev = near_ref.shape[0], keys_ref.shape[0]
    group = rows // q_tok
    scale = HD ** (-0.5)
    start, limit, seq_at = place_ref[0], place_ref[1], place_ref[2]
    near_query = near_ref[...]
    far_query = far_ref[...]
    token = lax.broadcasted_iota(jnp.int32, (rows, ctx_dev), 0) & (q_tok - 1)
    key_pos = start + lax.broadcasted_iota(jnp.int32, (rows, ctx_dev), 1)
    distance = context + token - key_pos
    near = dot_rows(near_query, rotated_ref[...])
    far = dot_rows(far_query, keys_ref[...])
    score = jnp.where(distance < limit, near, far) * scale
    distance = (lax.broadcasted_iota(jnp.int32, (rows, 1), 0) & (q_tok - 1)) - seq_at
    fresh_rotated = fresh_rotated_ref[...].astype(jnp.float32)
    fresh_key = fresh_key_ref[...].astype(jnp.float32)
    near = jnp.sum(near_query.astype(jnp.float32) * fresh_rotated, axis=1, keepdims=True)
    far = jnp.sum(far_query.astype(jnp.float32) * fresh_key, axis=1, keepdims=True)
    fresh = jnp.where(distance < limit, near, far) * scale
    fresh = jnp.where(distance >= 0, fresh, MASKED)
    high = jnp.maximum(jnp.max(score, axis=1, keepdims=True), fresh)
    high = high.astype(jnp.bfloat16).astype(jnp.float32)
    expo = jnp.exp(score - high)
    fresh = jnp.exp(fresh - high)
    total = jnp.sum(expo, axis=1, keepdims=True) + fresh
    sums = dot(expo.astype(jnp.bfloat16), values_ref[...])
    fresh = fresh.astype(jnp.bfloat16).astype(jnp.float32)
    sums = sums + fresh * fresh_value_ref[...].astype(jnp.float32)
    total_high = total.astype(jnp.bfloat16).astype(jnp.float32)
    total_low = total - total_high
    lane = lax.broadcasted_iota(jnp.int32, (q_tok, HD), 1)
    facts = jnp.zeros((q_tok, HD), jnp.float32)
    for h in range(group):
        part = slice(h * q_tok, (h + 1) * q_tok)
        wide_ref[:, h, :] = sums[part]
        facts = jnp.where(lane == h, high[part], facts)
        facts = jnp.where(lane == group + h, total_high[part], facts)
        facts = jnp.where(lane == 2 * group + h, total_low[part], facts)
    wide_ref[:, group, :] = facts
    wide_ref[:, group + 1, :] = jnp.zeros((q_tok, HD), jnp.float32)
    out_ref[...] = wide_ref[...].astype(out_ref.dtype)


def attend(context, q_tok, place, *arrays):
    rows = arrays[0].shape[0] // q_tok + 2
    vmem = pl.BlockSpec(memory_space=pltpu.VMEM)
    smem = pl.BlockSpec(memory_space=pltpu.SMEM)
    return pl.pallas_call(
        functools.partial(attend_kernel, context),
        out_shape=(
            jax.ShapeDtypeStruct((q_tok, rows, HD), jnp.bfloat16),
            jax.ShapeDtypeStruct((2,), jnp.int32),
            jax.ShapeDtypeStruct(arrays[-2].shape, arrays[-2].dtype),
            jax.ShapeDtypeStruct(arrays[-1].shape, arrays[-1].dtype),
        ),
        in_specs=[smem] + [vmem] * len(arrays),
        out_specs=(vmem, smem, vmem, vmem),
        scratch_shapes=[pltpu.VMEM((q_tok, rows, HD), jnp.float32)],
        compiler_params=pltpu.CompilerParams(vmem_limit_bytes=16 << 20),
    )(place, *arrays)


def expert_kernel(
    gain_row,
    place_ref,
    mine_ref,
    other_ref,
    w_gate,
    w_up,
    w_down,
    tokens_ref,
    kept_ref,
    sent_ref,
    own_ref,
    gate_ref,
    up_ref,
    down_ref,
    sems,
):
    rows, half = mine_ref.shape
    depth = w_gate.shape[0]
    steps = 4
    width = half // steps
    core = place_ref[0]
    own_ref[...] = tokens_ref[place_ref[1]].astype(own_ref.dtype)
    copies = []
    for i in range(steps):
        part = pl.ds(i * (depth // steps), depth // steps)
        for j, (source, target) in enumerate(((w_gate, gate_ref), (w_up, up_ref))):
            copy = pltpu.make_async_copy(source.at[part], target.at[part], sems.at[2 * i + j])
            copy.start()
            copies.append(copy)
    last = pltpu.make_async_copy(w_down, down_ref, sems.at[2 * steps])
    last.start()

    mine = mine_ref[...].astype(jnp.float32)
    other = other_ref[...].astype(jnp.float32)
    squares = jnp.sum(mine * mine, axis=1, keepdims=True)
    squares = squares + jnp.sum(other * other, axis=1, keepdims=True)
    scale = lax.rsqrt(squares / D + NORM_EPS)
    mine = (mine * scale * mine[gain_row : gain_row + 1]).astype(jnp.bfloat16)
    other = (other * scale * other[gain_row : gain_row + 1]).astype(jnp.bfloat16)
    gate = jnp.zeros((rows, gate_ref.shape[1]), jnp.float32)
    upward = gate
    for i in range(steps):
        copies[2 * i].wait()
        copies[2 * i + 1].wait()
        for side, values in ((core, mine), (1 - core, other)):
            part = pl.ds(pl.multiple_of((2 * i + side) * width, width), width)
            block = values[:, i * width : (i + 1) * width]
            gate = gate + dot(block, gate_ref[part, :])
            upward = upward + dot(block, up_ref[part, :])
    hidden = (gate / (1.0 + jnp.exp(-gate)) * upward).astype(jnp.bfloat16)
    last.wait()
    for i in range(steps):
        part = pl.ds(pl.multiple_of((2 * i + 1 - core) * width, width), width)
        columns = slice(i * width, (i + 1) * width)
        sent_ref[:, columns] = dot(hidden, down_ref[:, part]).astype(sent_ref.dtype)
        part = pl.ds(pl.multiple_of((2 * i + core) * width, width), width)
        kept_ref[:, columns] = dot(hidden, down_ref[:, part])


def feed(gain_row, place, mine, other, w_gate, w_up, w_down, tokens):
    vmem = pl.BlockSpec(memory_space=pltpu.VMEM)
    far_memory = pl.BlockSpec(memory_space=pltpu.HBM)
    return pl.pallas_call(
        functools.partial(expert_kernel, gain_row),
        out_shape=(
            jax.ShapeDtypeStruct(mine.shape, jnp.float32),
            jax.ShapeDtypeStruct(mine.shape, jnp.bfloat16),
            jax.ShapeDtypeStruct(tokens.shape[1:], jnp.float32),
        ),
        in_specs=[pl.BlockSpec(memory_space=pltpu.SMEM), vmem, vmem] + [far_memory] * 3 + [vmem],
        out_specs=(vmem, vmem, vmem),
        scratch_shapes=[
            pltpu.VMEM(w_gate.shape, w_gate.dtype),
            pltpu.VMEM(w_up.shape, w_up.dtype),
            pltpu.VMEM(w_down.shape, w_down.dtype),
            pltpu.SemaphoreType.DMA((9,)),
        ],
        compiler_params=pltpu.CompilerParams(vmem_limit_bytes=52 << 20),
    )(place, mine, other, w_gate, w_up, w_down, tokens)


def swap(value, axis, mask):
    size = lax.axis_size(axis)
    return lax.ppermute(value, axis, [(i, i ^ mask) for i in range(size)])


def exchange(value, axis, groups=None):
    return lax.all_to_all(value, axis, 0, 0, axis_index_groups=groups, tiled=True)


def spread(value, axis, count, groups=None):
    return exchange(jnp.broadcast_to(value[None], (count, *value.shape)), axis, groups)


def local(
    queries,
    key_cache,
    value_cache,
    key_new,
    value_new,
    window,
    norm_gain,
    expert_ids,
    gate_values,
    w_gate,
    w_up,
    w_down,
):
    seq_count = lax.axis_size("seq")
    exp_count = lax.axis_size("exp")
    seq_at = lax.axis_index("seq")
    exp_at = lax.axis_index("exp")
    group = HEADS // KV_HEADS
    width = group * HD
    ctx_dev = key_cache.shape[0]
    q_tok = seq_count
    context = ctx_dev * seq_count
    freq = frequencies(HD)
    limit = window[0]
    quarter = exp_count // 2
    core = exp_at % 2
    run = seq_count // 16
    plane = seq_count // run
    flat = [[run * i + j for i in range(plane)] for j in range(run)]
    tall = [
        [(run * i + j) * exp_count + 2 * h + c for j in range(run) for h in range(quarter)]
        for i in range(plane)
        for c in range(2)
    ]

    stretch = exchange(row_copies(queries, seq_count, group), "seq")
    query_pos = context + jnp.arange(q_tok, dtype=jnp.int32)
    query_f32 = stretch.astype(jnp.float32)
    near_query = rotate(
        query_f32, query_pos.astype(jnp.float32)[:, None, None] * freq
    ).astype(jnp.bfloat16)
    far_query = rotate(query_f32, limit.astype(jnp.float32) * freq).astype(jnp.bfloat16)
    near_query = jnp.transpose(near_query, (1, 0, 2)).reshape(group * q_tok, HD)
    far_query = jnp.transpose(far_query, (1, 0, 2)).reshape(group * q_tok, HD)
    key_pos = seq_at * ctx_dev + jnp.arange(ctx_dev, dtype=jnp.int32)
    rotated_cache = rotate(
        key_cache.astype(jnp.float32), key_pos.astype(jnp.float32)[:, None] * freq
    ).astype(jnp.bfloat16)
    rotated_fresh = rotate(
        key_new.astype(jnp.float32), (context + seq_at).astype(jnp.float32) * freq
    ).astype(jnp.bfloat16)
    ff_dev = w_gate.shape[1]
    expert = (seq_at * exp_count + exp_at) * ff_dev // FF
    capacity = (q_tok * 17 + 31) // 32
    matched = (expert_ids == expert).astype(jnp.int32)
    chosen = jnp.sum(matched, axis=1)
    weight = jnp.sum(gate_values * matched.astype(jnp.float32), axis=1)
    slot = jnp.cumsum(chosen) - chosen
    gain_row = -(-capacity // 8) * 8
    rows = jnp.arange(-(-(gain_row + 1) // 16) * 16, dtype=jnp.int32)[:, None]
    dispatch = (slot[None, :] == rows) & (rows < capacity) & (
        chosen[None, :] == 1
    )
    row_weight = jnp.sum(jnp.where(dispatch, weight[None, :], 0.0), axis=1, keepdims=True)
    dispatch = dispatch.astype(jnp.bfloat16)

    place = jnp.stack(
        [seq_at * ctx_dev, limit, seq_at, core, seq_at % run * quarter + exp_at // 2]
    )
    parts, later, dispatch, row_weight = attend(
        context,
        q_tok,
        place,
        near_query,
        far_query,
        rotated_cache,
        key_cache,
        value_cache,
        rotated_fresh,
        key_new,
        value_new,
        dispatch,
        row_weight,
    )

    parts = exchange(parts.reshape(plane, run, group + 2, HD), "seq", flat)
    parts = parts.astype(jnp.float32)
    maxima = parts[:, :, group, :group]
    totals = parts[:, :, group, group : 2 * group] + parts[:, :, group, 2 * group : 3 * group]
    top = jnp.max(maxima, axis=0)
    weights = jnp.exp(maxima - top)
    total = jnp.sum(weights * totals, axis=0)
    sums = jnp.sum(weights[..., None] * parts[:, :, :group, :], axis=0).astype(jnp.bfloat16)
    total_high = total.astype(jnp.bfloat16)
    total_low = (total - total_high.astype(jnp.float32)).astype(jnp.bfloat16)
    facts = jnp.concatenate(
        [top.astype(jnp.bfloat16).ravel(), total_high.ravel(), total_low.ravel()]
    )
    facts = jnp.pad(facts, (0, HD - facts.shape[0]))[None]
    lines = jnp.concatenate(
        [
            sums.reshape(run * group, HD),
            facts,
            norm_gain.reshape(group, HD),
            facts,
        ]
    )
    lines = spread(lines, ("seq", "exp"), run * quarter, tall)
    lines = lines.reshape(run, quarter, -1, HD)
    gain = lines[0, :, run * group + 1 : run * group + 1 + group]
    facts = lines[:, :, run * group, : 3 * run * group].astype(jnp.float32)
    facts = facts.reshape(run, quarter, 3, run, group)
    weights = jnp.exp(facts[:, :, 0] - jnp.max(facts[:, :, 0], axis=0))
    below = jnp.sum(weights * (facts[:, :, 1] + facts[:, :, 2]), axis=0)
    sums = lines[:, :, : run * group].astype(jnp.float32).reshape(run, quarter, run, group, HD)
    above = jnp.sum(weights[..., None] * sums, axis=0)
    attention = (above / below[..., None]).astype(jnp.bfloat16)
    attention = jnp.transpose(attention, (1, 0, 2, 3))

    tokens = spread(attention.reshape(run, quarter * group, HD), "seq", plane, flat)
    tokens = tokens.reshape(q_tok, quarter * width)
    routed = dot(dispatch, tokens).astype(jnp.bfloat16)
    mine = jnp.concatenate(
        [routed[:gain_row], gain.reshape(1, quarter * width), routed[gain_row + 1 :]]
    )
    other = swap(mine, "exp", 1)
    kept, sent, own = feed(
        gain_row,
        later,
        mine,
        other,
        w_gate,
        w_up,
        w_down,
        attention.reshape(run * quarter, group, HD),
    )

    half = kept + swap(sent, "exp", 1).astype(jnp.float32)
    half = (half * row_weight).astype(jnp.bfloat16)
    rows = jnp.dot(dispatch.T, half, preferred_element_type=jnp.float32).astype(jnp.bfloat16)
    rows = exchange(rows.reshape(plane, run, quarter * group, HD), "seq", flat)
    rows = jnp.sum(rows.astype(jnp.float32), axis=0).astype(jnp.bfloat16)
    rows = exchange(rows.reshape(run * quarter, group, HD), ("seq", "exp"), tall)
    expert_rows = jnp.sum(rows.astype(jnp.float32), axis=0)
    return (own + expert_rows).astype(jnp.bfloat16).reshape(1, width)


def solution(mesh):
    in_specs = (
        P("seq", "exp"),
        P("seq", "exp"),
        P("seq", "exp"),
        P("seq", "exp"),
        P("seq", "exp"),
        P(),
        P("exp"),
        P(),
        P(),
        P(None, ("seq", "exp")),
        P(None, ("seq", "exp")),
        P(("seq", "exp"), None),
    )
    out_specs = P("seq", "exp")
    return jax.shard_map(local, mesh=mesh, in_specs=in_specs, out_specs=out_specs, check_vma=False)
```

```python
import functools

import jax
import jax.numpy as jnp
from jax import lax
from jax.experimental import pallas as pl
from jax.experimental.pallas import tpu as pltpu
from jax.sharding import PartitionSpec as P

D = 6144
HEADS = 48
KV_HEADS = 8
HD = 128
FF = 16384


ROPE_BASE = 1000000.0
NORM_EPS = 1e-05
MASKED = -1e30


def frequencies(width):
    index = jnp.arange(width // 2, dtype=jnp.float32)
    return ROPE_BASE ** (-2.0 * index / width)


def rotate(values, angles):
    half = values.shape[-1] // 2
    first = values[..., :half]
    second = values[..., half:]
    cosine = jnp.cos(angles)
    sine = jnp.sin(angles)
    return jnp.concatenate(
        [first * cosine - second * sine, second * cosine + first * sine], axis=-1
    )


def dot(left, right):
    return jnp.dot(left, right, preferred_element_type=jnp.float32)


def dot_rows(left, right):
    return lax.dot_general(
        left, right, (((1,), (1,)), ((), ())), preferred_element_type=jnp.float32
    )


def copies_kernel(row_ref, out_ref):
    group = out_ref.shape[1]
    row = row_ref[...].astype(jnp.float32)
    block = jnp.concatenate([row[:, h * HD : (h + 1) * HD] for h in range(group)], 0)
    out_ref[...] = jnp.broadcast_to(block[None], out_ref.shape).astype(out_ref.dtype)


def row_copies(row, count, group):
    return pl.pallas_call(
        copies_kernel,
        out_shape=jax.ShapeDtypeStruct((count, group, HD), row.dtype),
    )(row)


def attend_kernel(
    context,
    place_ref,
    near_ref,
    far_ref,
    rotated_ref,
    keys_ref,
    values_ref,
    fresh_rotated_ref,
    fresh_key_ref,
    fresh_value_ref,
    dispatch_ref,
    weight_ref,
    out_ref,
    later_ref,
    dispatch_out_ref,
    weight_out_ref,
    wide_ref,
):
    later_ref[0] = place_ref[3]
    later_ref[1] = place_ref[4]
    dispatch_out_ref[...] = dispatch_ref[...]
    weight_out_ref[...] = weight_ref[...]
    q_tok = out_ref.shape[0]
    rows, ctx_dev = near_ref.shape[0], keys_ref.shape[0]
    group = rows // q_tok
    scale = HD ** (-0.5)
    start, limit, seq_at = place_ref[0], place_ref[1], place_ref[2]
    near_query = near_ref[...]
    far_query = far_ref[...]
    token = lax.broadcasted_iota(jnp.int32, (rows, ctx_dev), 0) & (q_tok - 1)
    key_pos = start + lax.broadcasted_iota(jnp.int32, (rows, ctx_dev), 1)
    distance = context + token - key_pos
    near = dot_rows(near_query, rotated_ref[...])
    far = dot_rows(far_query, keys_ref[...])
    score = jnp.where(distance < limit, near, far) * scale
    distance = (lax.broadcasted_iota(jnp.int32, (rows, 1), 0) & (q_tok - 1)) - seq_at
    fresh_rotated = fresh_rotated_ref[...].astype(jnp.float32)
    fresh_key = fresh_key_ref[...].astype(jnp.float32)
    near = jnp.sum(near_query.astype(jnp.float32) * fresh_rotated, axis=1, keepdims=True)
    far = jnp.sum(far_query.astype(jnp.float32) * fresh_key, axis=1, keepdims=True)
    fresh = jnp.where(distance < limit, near, far) * scale
    fresh = jnp.where(distance >= 0, fresh, MASKED)
    high = jnp.maximum(jnp.max(score, axis=1, keepdims=True), fresh)
    high = high.astype(jnp.bfloat16).astype(jnp.float32)
    expo = jnp.exp(score - high)
    fresh = jnp.exp(fresh - high)
    total = jnp.sum(expo, axis=1, keepdims=True) + fresh
    sums = dot(expo.astype(jnp.bfloat16), values_ref[...])
    fresh = fresh.astype(jnp.bfloat16).astype(jnp.float32)
    sums = sums + fresh * fresh_value_ref[...].astype(jnp.float32)
    total_high = total.astype(jnp.bfloat16).astype(jnp.float32)
    total_low = total - total_high
    lane = lax.broadcasted_iota(jnp.int32, (q_tok, HD), 1)
    facts = jnp.zeros((q_tok, HD), jnp.float32)
    for h in range(group):
        part = slice(h * q_tok, (h + 1) * q_tok)
        wide_ref[:, h, :] = sums[part]
        facts = jnp.where(lane == h, high[part], facts)
        facts = jnp.where(lane == group + h, total_high[part], facts)
        facts = jnp.where(lane == 2 * group + h, total_low[part], facts)
    wide_ref[:, group, :] = facts
    wide_ref[:, group + 1, :] = jnp.zeros((q_tok, HD), jnp.float32)
    out_ref[...] = wide_ref[...].astype(out_ref.dtype)


def attend(context, q_tok, place, *arrays):
    rows = arrays[0].shape[0] // q_tok + 2
    vmem = pl.BlockSpec(memory_space=pltpu.VMEM)
    smem = pl.BlockSpec(memory_space=pltpu.SMEM)
    return pl.pallas_call(
        functools.partial(attend_kernel, context),
        out_shape=(
            jax.ShapeDtypeStruct((q_tok, rows, HD), jnp.bfloat16),
            jax.ShapeDtypeStruct((2,), jnp.int32),
            jax.ShapeDtypeStruct(arrays[-2].shape, arrays[-2].dtype),
            jax.ShapeDtypeStruct(arrays[-1].shape, arrays[-1].dtype),
        ),
        in_specs=[smem] + [vmem] * len(arrays),
        out_specs=(vmem, smem, vmem, vmem),
        scratch_shapes=[pltpu.VMEM((q_tok, rows, HD), jnp.float32)],
        compiler_params=pltpu.CompilerParams(vmem_limit_bytes=16 << 20),
    )(place, *arrays)


def expert_kernel(
    gain_row,
    place_ref,
    mine_ref,
    other_ref,
    w_gate,
    w_up,
    w_down,
    tokens_ref,
    kept_ref,
    sent_ref,
    own_ref,
    gate_ref,
    up_ref,
    down_ref,
    sems,
):
    rows, half = mine_ref.shape
    depth = w_gate.shape[0]
    steps = 4
    width = half // steps
    core = place_ref[0]
    own_ref[...] = tokens_ref[place_ref[1]].astype(own_ref.dtype)
    copies = []
    for i in range(steps):
        part = pl.ds(i * (depth // steps), depth // steps)
        for j, (source, target) in enumerate(((w_gate, gate_ref), (w_up, up_ref))):
            copy = pltpu.make_async_copy(source.at[part], target.at[part], sems.at[2 * i + j])
            copy.start()
            copies.append(copy)
    last = pltpu.make_async_copy(w_down, down_ref, sems.at[2 * steps])
    last.start()

    mine = mine_ref[...].astype(jnp.float32)
    other = other_ref[...].astype(jnp.float32)
    squares = jnp.sum(mine * mine, axis=1, keepdims=True)
    squares = squares + jnp.sum(other * other, axis=1, keepdims=True)
    scale = lax.rsqrt(squares / D + NORM_EPS)
    mine = (mine * scale * mine[gain_row : gain_row + 1]).astype(jnp.bfloat16)
    other = (other * scale * other[gain_row : gain_row + 1]).astype(jnp.bfloat16)
    gate = jnp.zeros((rows, gate_ref.shape[1]), jnp.float32)
    upward = gate
    for i in range(steps):
        copies[2 * i].wait()
        copies[2 * i + 1].wait()
        for side, values in ((core, mine), (1 - core, other)):
            part = pl.ds(pl.multiple_of((2 * i + side) * width, width), width)
            block = values[:, i * width : (i + 1) * width]
            gate = gate + dot(block, gate_ref[part, :])
            upward = upward + dot(block, up_ref[part, :])
    hidden = (gate / (1.0 + jnp.exp(-gate)) * upward).astype(jnp.bfloat16)
    last.wait()
    for i in range(steps):
        part = pl.ds(pl.multiple_of((2 * i + 1 - core) * width, width), width)
        columns = slice(i * width, (i + 1) * width)
        sent_ref[:, columns] = dot(hidden, down_ref[:, part]).astype(sent_ref.dtype)
        part = pl.ds(pl.multiple_of((2 * i + core) * width, width), width)
        kept_ref[:, columns] = dot(hidden, down_ref[:, part])


def feed(gain_row, place, mine, other, w_gate, w_up, w_down, tokens):
    vmem = pl.BlockSpec(memory_space=pltpu.VMEM)
    far_memory = pl.BlockSpec(memory_space=pltpu.HBM)
    return pl.pallas_call(
        functools.partial(expert_kernel, gain_row),
        out_shape=(
            jax.ShapeDtypeStruct(mine.shape, jnp.float32),
            jax.ShapeDtypeStruct(mine.shape, jnp.bfloat16),
            jax.ShapeDtypeStruct(tokens.shape[1:], jnp.float32),
        ),
        in_specs=[pl.BlockSpec(memory_space=pltpu.SMEM), vmem, vmem] + [far_memory] * 3 + [vmem],
        out_specs=(vmem, vmem, vmem),
        scratch_shapes=[
            pltpu.VMEM(w_gate.shape, w_gate.dtype),
            pltpu.VMEM(w_up.shape, w_up.dtype),
            pltpu.VMEM(w_down.shape, w_down.dtype),
            pltpu.SemaphoreType.DMA((9,)),
        ],
        compiler_params=pltpu.CompilerParams(vmem_limit_bytes=52 << 20),
    )(place, mine, other, w_gate, w_up, w_down, tokens)


def swap(value, axis, mask):
    size = lax.axis_size(axis)
    return lax.ppermute(value, axis, [(i, i ^ mask) for i in range(size)])


def exchange(value, axis, groups=None):
    return lax.all_to_all(value, axis, 0, 0, axis_index_groups=groups, tiled=True)


def spread(value, axis, count, groups=None):
    return exchange(jnp.broadcast_to(value[None], (count, *value.shape)), axis, groups)


def local(
    queries,
    key_cache,
    value_cache,
    key_new,
    value_new,
    window,
    norm_gain,
    expert_ids,
    gate_values,
    w_gate,
    w_up,
    w_down,
):
    seq_count = lax.axis_size("seq")
    exp_count = lax.axis_size("exp")
    seq_at = lax.axis_index("seq")
    exp_at = lax.axis_index("exp")
    group = HEADS // KV_HEADS
    width = group * HD
    ctx_dev = key_cache.shape[0]
    q_tok = seq_count
    context = ctx_dev * seq_count
    freq = frequencies(HD)
    limit = window[0]
    quarter = exp_count // 2
    core = exp_at % 2
    run = seq_count // 16
    plane = seq_count // run
    flat = [[run * i + j for i in range(plane)] for j in range(run)]
    tall = [
        [(run * i + j) * exp_count + 2 * h + c for j in range(run) for h in range(quarter)]
        for i in range(plane)
        for c in range(2)
    ]

    stretch = exchange(row_copies(queries, seq_count, group), "seq")
    query_pos = context + jnp.arange(q_tok, dtype=jnp.int32)
    query_f32 = stretch.astype(jnp.float32)
    near_query = rotate(
        query_f32, query_pos.astype(jnp.float32)[:, None, None] * freq
    ).astype(jnp.bfloat16)
    far_query = rotate(query_f32, limit.astype(jnp.float32) * freq).astype(jnp.bfloat16)
    near_query = jnp.transpose(near_query, (1, 0, 2)).reshape(group * q_tok, HD)
    far_query = jnp.transpose(far_query, (1, 0, 2)).reshape(group * q_tok, HD)
    key_pos = seq_at * ctx_dev + jnp.arange(ctx_dev, dtype=jnp.int32)
    rotated_cache = rotate(
        key_cache.astype(jnp.float32), key_pos.astype(jnp.float32)[:, None] * freq
    ).astype(jnp.bfloat16)
    rotated_fresh = rotate(
        key_new.astype(jnp.float32), (context + seq_at).astype(jnp.float32) * freq
    ).astype(jnp.bfloat16)
    ff_dev = w_gate.shape[1]
    expert = (seq_at * exp_count + exp_at) * ff_dev // FF
    capacity = (q_tok * 17 + 31) // 32
    matched = (expert_ids == expert).astype(jnp.int32)
    chosen = jnp.sum(matched, axis=1)
    weight = jnp.sum(gate_values * matched.astype(jnp.float32), axis=1)
    slot = jnp.cumsum(chosen) - chosen
    gain_row = -(-(capacity + 1) // 8) * 8 - 1
    rows = jnp.arange(gain_row + 1, dtype=jnp.int32)[:, None]
    dispatch = (slot[None, :] == rows) & (rows < capacity) & (
        chosen[None, :] == 1
    )
    row_weight = jnp.sum(jnp.where(dispatch, weight[None, :], 0.0), axis=1, keepdims=True)
    dispatch = dispatch.astype(jnp.bfloat16)

    place = jnp.stack(
        [seq_at * ctx_dev, limit, seq_at, core, seq_at % run * quarter + exp_at // 2]
    )
    parts, later, dispatch, row_weight = attend(
        context,
        q_tok,
        place,
        near_query,
        far_query,
        rotated_cache,
        key_cache,
        value_cache,
        rotated_fresh,
        key_new,
        value_new,
        dispatch,
        row_weight,
    )

    parts = exchange(parts.reshape(plane, run, group + 2, HD), "seq", flat)
    parts = parts.astype(jnp.float32)
    maxima = parts[:, :, group, :group]
    totals = parts[:, :, group, group : 2 * group] + parts[:, :, group, 2 * group : 3 * group]
    top = jnp.max(maxima, axis=0)
    weights = jnp.exp(maxima - top)
    total = jnp.sum(weights * totals, axis=0)
    sums = jnp.sum(weights[..., None] * parts[:, :, :group, :], axis=0).astype(jnp.bfloat16)
    total_high = total.astype(jnp.bfloat16)
    total_low = (total - total_high.astype(jnp.float32)).astype(jnp.bfloat16)
    facts = jnp.concatenate(
        [top.astype(jnp.bfloat16).ravel(), total_high.ravel(), total_low.ravel()]
    )
    facts = jnp.pad(facts, (0, HD - facts.shape[0]))[None]
    lines = jnp.concatenate(
        [
            sums.reshape(run * group, HD),
            facts,
            norm_gain.reshape(group, HD),
            facts,
        ]
    )
    lines = spread(lines, ("seq", "exp"), run * quarter, tall)
    lines = lines.reshape(run, quarter, -1, HD)
    gain = lines[0, :, run * group + 1 : run * group + 1 + group]
    facts = lines[:, :, run * group, : 3 * run * group].astype(jnp.float32)
    facts = facts.reshape(run, quarter, 3, run, group)
    weights = jnp.exp(facts[:, :, 0] - jnp.max(facts[:, :, 0], axis=0))
    below = jnp.sum(weights * (facts[:, :, 1] + facts[:, :, 2]), axis=0)
    sums = lines[:, :, : run * group].astype(jnp.float32).reshape(run, quarter, run, group, HD)
    above = jnp.sum(weights[..., None] * sums, axis=0)
    attention = (above / below[..., None]).astype(jnp.bfloat16)
    attention = jnp.transpose(attention, (1, 0, 2, 3))

    tokens = spread(attention.reshape(run, quarter * group, HD), "seq", plane, flat)
    tokens = tokens.reshape(q_tok, quarter * width)
    routed = dot(dispatch, tokens).astype(jnp.bfloat16)
    mine = jnp.concatenate([routed[:gain_row], gain.reshape(1, quarter * width)])
    other = swap(mine, "exp", 1)
    kept, sent, own = feed(
        gain_row,
        later,
        mine,
        other,
        w_gate,
        w_up,
        w_down,
        attention.reshape(run * quarter, group, HD),
    )

    half = kept + swap(sent, "exp", 1).astype(jnp.float32)
    half = (half * row_weight).astype(jnp.bfloat16)
    rows = jnp.dot(dispatch.T, half, preferred_element_type=jnp.float32).astype(jnp.bfloat16)
    rows = exchange(rows.reshape(plane, run, quarter * group, HD), "seq", flat)
    rows = jnp.sum(rows.astype(jnp.float32), axis=0).astype(jnp.bfloat16)
    rows = exchange(rows.reshape(run * quarter, group, HD), ("seq", "exp"), tall)
    expert_rows = jnp.sum(rows.astype(jnp.float32), axis=0)
    return (own + expert_rows).astype(jnp.bfloat16).reshape(1, width)


def solution(mesh):
    in_specs = (
        P("seq", "exp"),
        P("seq", "exp"),
        P("seq", "exp"),
        P("seq", "exp"),
        P("seq", "exp"),
        P(),
        P("exp"),
        P(),
        P(),
        P(None, ("seq", "exp")),
        P(None, ("seq", "exp")),
        P(("seq", "exp"), None),
    )
    out_specs = P("seq", "exp")
    return jax.shard_map(local, mesh=mesh, in_specs=in_specs, out_specs=out_specs, check_vma=False)
```

```python
import functools

import jax
import jax.numpy as jnp
from jax import lax
from jax.experimental import pallas as pl
from jax.experimental.pallas import tpu as pltpu
from jax.sharding import PartitionSpec as P

D = 6144
HEADS = 48
KV_HEADS = 8
HD = 128
FF = 16384


ROPE_BASE = 1000000.0
NORM_EPS = 1e-05
MASKED = -1e30


def frequencies(width):
    index = jnp.arange(width // 2, dtype=jnp.float32)
    return ROPE_BASE ** (-2.0 * index / width)


def rotate(values, angles):
    half = values.shape[-1] // 2
    first = values[..., :half]
    second = values[..., half:]
    cosine = jnp.cos(angles)
    sine = jnp.sin(angles)
    return jnp.concatenate(
        [first * cosine - second * sine, second * cosine + first * sine], axis=-1
    )


def dot(left, right):
    return jnp.dot(left, right, preferred_element_type=jnp.float32)


def dot_rows(left, right):
    return lax.dot_general(
        left, right, (((1,), (1,)), ((), ())), preferred_element_type=jnp.float32
    )


def copies_kernel(row_ref, out_ref):
    group = out_ref.shape[1]
    row = row_ref[...].astype(jnp.float32)
    block = jnp.concatenate([row[:, h * HD : (h + 1) * HD] for h in range(group)], 0)
    out_ref[...] = jnp.broadcast_to(block[None], out_ref.shape).astype(out_ref.dtype)


def row_copies(row, count, group):
    return pl.pallas_call(
        copies_kernel,
        out_shape=jax.ShapeDtypeStruct((count, group, HD), row.dtype),
    )(row)


def attend_kernel(
    context,
    place_ref,
    near_ref,
    far_ref,
    rotated_ref,
    keys_ref,
    values_ref,
    fresh_rotated_ref,
    fresh_key_ref,
    fresh_value_ref,
    dispatch_ref,
    weight_ref,
    out_ref,
    later_ref,
    dispatch_out_ref,
    weight_out_ref,
    wide_ref,
):
    later_ref[0] = place_ref[3]
    later_ref[1] = place_ref[4]
    dispatch_out_ref[...] = dispatch_ref[...]
    weight_out_ref[...] = weight_ref[...]
    q_tok = out_ref.shape[0]
    rows, ctx_dev = near_ref.shape[0], keys_ref.shape[0]
    group = rows // q_tok
    scale = HD ** (-0.5)
    start, limit, seq_at = place_ref[0], place_ref[1], place_ref[2]
    near_query = near_ref[...]
    far_query = far_ref[...]
    token = lax.broadcasted_iota(jnp.int32, (rows, ctx_dev), 0) & (q_tok - 1)
    key_pos = start + lax.broadcasted_iota(jnp.int32, (rows, ctx_dev), 1)
    distance = context + token - key_pos
    near = dot_rows(near_query, rotated_ref[...])
    far = dot_rows(far_query, keys_ref[...])
    score = jnp.where(distance < limit, near, far) * scale
    distance = (lax.broadcasted_iota(jnp.int32, (rows, 1), 0) & (q_tok - 1)) - seq_at
    fresh_rotated = fresh_rotated_ref[...].astype(jnp.float32)
    fresh_key = fresh_key_ref[...].astype(jnp.float32)
    near = jnp.sum(near_query.astype(jnp.float32) * fresh_rotated, axis=1, keepdims=True)
    far = jnp.sum(far_query.astype(jnp.float32) * fresh_key, axis=1, keepdims=True)
    fresh = jnp.where(distance < limit, near, far) * scale
    fresh = jnp.where(distance >= 0, fresh, MASKED)
    high = jnp.maximum(jnp.max(score, axis=1, keepdims=True), fresh)
    high = high.astype(jnp.bfloat16).astype(jnp.float32)
    expo = jnp.exp(score - high)
    fresh = jnp.exp(fresh - high)
    total = jnp.sum(expo, axis=1, keepdims=True) + fresh
    sums = dot(expo.astype(jnp.bfloat16), values_ref[...])
    fresh = fresh.astype(jnp.bfloat16).astype(jnp.float32)
    sums = sums + fresh * fresh_value_ref[...].astype(jnp.float32)
    total_high = total.astype(jnp.bfloat16).astype(jnp.float32)
    total_low = total - total_high
    lane = lax.broadcasted_iota(jnp.int32, (q_tok, HD), 1)
    facts = jnp.zeros((q_tok, HD), jnp.float32)
    for h in range(group):
        part = slice(h * q_tok, (h + 1) * q_tok)
        wide_ref[:, h, :] = sums[part]
        facts = jnp.where(lane == h, high[part], facts)
        facts = jnp.where(lane == group + h, total_high[part], facts)
        facts = jnp.where(lane == 2 * group + h, total_low[part], facts)
    wide_ref[:, group, :] = facts
    wide_ref[:, group + 1, :] = jnp.zeros((q_tok, HD), jnp.float32)
    out_ref[...] = wide_ref[...].astype(out_ref.dtype)


def attend(context, q_tok, place, *arrays):
    rows = arrays[0].shape[0] // q_tok + 2
    vmem = pl.BlockSpec(memory_space=pltpu.VMEM)
    smem = pl.BlockSpec(memory_space=pltpu.SMEM)
    return pl.pallas_call(
        functools.partial(attend_kernel, context),
        out_shape=(
            jax.ShapeDtypeStruct((q_tok, rows, HD), jnp.bfloat16),
            jax.ShapeDtypeStruct((2,), jnp.int32),
            jax.ShapeDtypeStruct(arrays[-2].shape, arrays[-2].dtype),
            jax.ShapeDtypeStruct(arrays[-1].shape, arrays[-1].dtype),
        ),
        in_specs=[smem] + [vmem] * len(arrays),
        out_specs=(vmem, smem, vmem, vmem),
        scratch_shapes=[pltpu.VMEM((q_tok, rows, HD), jnp.float32)],
        compiler_params=pltpu.CompilerParams(vmem_limit_bytes=16 << 20),
    )(place, *arrays)


def expert_kernel(
    gain_row,
    place_ref,
    mine_ref,
    other_ref,
    w_gate,
    w_up,
    w_down,
    tokens_ref,
    kept_ref,
    sent_ref,
    own_ref,
    gate_ref,
    up_ref,
    down_ref,
    sems,
):
    rows, half = mine_ref.shape
    depth = w_gate.shape[0]
    steps = 4
    width = half // steps
    core = place_ref[0]
    own_ref[...] = tokens_ref[place_ref[1]].astype(own_ref.dtype)
    copies = []
    for i in range(steps):
        part = pl.ds(i * (depth // steps), depth // steps)
        for j, (source, target) in enumerate(((w_gate, gate_ref), (w_up, up_ref))):
            copy = pltpu.make_async_copy(source.at[part], target.at[part], sems.at[2 * i + j])
            copy.start()
            copies.append(copy)
    last = pltpu.make_async_copy(w_down, down_ref, sems.at[2 * steps])
    last.start()

    mine = mine_ref[...].astype(jnp.float32)
    other = other_ref[...].astype(jnp.float32)
    squares = jnp.sum(mine * mine, axis=1, keepdims=True)
    squares = squares + jnp.sum(other * other, axis=1, keepdims=True)
    scale = lax.rsqrt(squares / D + NORM_EPS)
    mine = (mine * scale * mine[gain_row : gain_row + 1]).astype(jnp.bfloat16)
    other = (other * scale * other[gain_row : gain_row + 1]).astype(jnp.bfloat16)
    gate = jnp.zeros((rows, gate_ref.shape[1]), jnp.float32)
    upward = gate
    for i in range(steps):
        copies[2 * i].wait()
        copies[2 * i + 1].wait()
        for side, values in ((core, mine), (1 - core, other)):
            part = pl.ds(pl.multiple_of((2 * i + side) * width, width), width)
            block = values[:, i * width : (i + 1) * width]
            gate = gate + dot(block, gate_ref[part, :])
            upward = upward + dot(block, up_ref[part, :])
    hidden = (gate / (1.0 + jnp.exp(-gate)) * upward).astype(jnp.bfloat16)
    last.wait()
    for i in range(steps):
        part = pl.ds(pl.multiple_of((2 * i + 1 - core) * width, width), width)
        columns = slice(i * width, (i + 1) * width)
        sent_ref[:, columns] = dot(hidden, down_ref[:, part]).astype(sent_ref.dtype)
        part = pl.ds(pl.multiple_of((2 * i + core) * width, width), width)
        kept_ref[:, columns] = dot(hidden, down_ref[:, part])


def feed(gain_row, place, mine, other, w_gate, w_up, w_down, tokens):
    vmem = pl.BlockSpec(memory_space=pltpu.VMEM)
    far_memory = pl.BlockSpec(memory_space=pltpu.HBM)
    return pl.pallas_call(
        functools.partial(expert_kernel, gain_row),
        out_shape=(
            jax.ShapeDtypeStruct(mine.shape, jnp.float32),
            jax.ShapeDtypeStruct(mine.shape, jnp.bfloat16),
            jax.ShapeDtypeStruct(tokens.shape[1:], jnp.float32),
        ),
        in_specs=[pl.BlockSpec(memory_space=pltpu.SMEM), vmem, vmem] + [far_memory] * 3 + [vmem],
        out_specs=(vmem, vmem, vmem),
        scratch_shapes=[
            pltpu.VMEM(w_gate.shape, w_gate.dtype),
            pltpu.VMEM(w_up.shape, w_up.dtype),
            pltpu.VMEM(w_down.shape, w_down.dtype),
            pltpu.SemaphoreType.DMA((9,)),
        ],
        compiler_params=pltpu.CompilerParams(vmem_limit_bytes=52 << 20),
    )(place, mine, other, w_gate, w_up, w_down, tokens)


def swap(value, axis, mask):
    size = lax.axis_size(axis)
    return lax.ppermute(value, axis, [(i, i ^ mask) for i in range(size)])


def exchange(value, axis, groups=None):
    return lax.all_to_all(value, axis, 0, 0, axis_index_groups=groups, tiled=True)


def spread(value, axis, count, groups=None):
    return exchange(jnp.broadcast_to(value[None], (count, *value.shape)), axis, groups)


def local(
    queries,
    key_cache,
    value_cache,
    key_new,
    value_new,
    window,
    norm_gain,
    expert_ids,
    gate_values,
    w_gate,
    w_up,
    w_down,
):
    seq_count = lax.axis_size("seq")
    exp_count = lax.axis_size("exp")
    seq_at = lax.axis_index("seq")
    exp_at = lax.axis_index("exp")
    group = HEADS // KV_HEADS
    width = group * HD
    ctx_dev = key_cache.shape[0]
    q_tok = seq_count
    context = ctx_dev * seq_count
    freq = frequencies(HD)
    limit = window[0]
    quarter = exp_count // 2
    core = exp_at % 2
    run = seq_count // 16
    plane = seq_count // run
    flat = [[run * i + j for i in range(plane)] for j in range(run)]
    tall = [
        [(run * i + j) * exp_count + 2 * h + c for j in range(run) for h in range(quarter)]
        for i in range(plane)
        for c in range(2)
    ]

    stretch = exchange(row_copies(queries, seq_count, group), "seq")
    query_pos = context + jnp.arange(q_tok, dtype=jnp.int32)
    query_f32 = stretch.astype(jnp.float32)
    near_query = rotate(
        query_f32, query_pos.astype(jnp.float32)[:, None, None] * freq
    ).astype(jnp.bfloat16)
    far_query = rotate(query_f32, limit.astype(jnp.float32) * freq).astype(jnp.bfloat16)
    near_query = jnp.transpose(near_query, (1, 0, 2)).reshape(group * q_tok, HD)
    far_query = jnp.transpose(far_query, (1, 0, 2)).reshape(group * q_tok, HD)
    key_pos = seq_at * ctx_dev + jnp.arange(ctx_dev, dtype=jnp.int32)
    rotated_cache = rotate(
        key_cache.astype(jnp.float32), key_pos.astype(jnp.float32)[:, None] * freq
    ).astype(jnp.bfloat16)
    rotated_fresh = rotate(
        key_new.astype(jnp.float32), (context + seq_at).astype(jnp.float32) * freq
    ).astype(jnp.bfloat16)
    ff_dev = w_gate.shape[1]
    expert = (seq_at * exp_count + exp_at) * ff_dev // FF
    capacity = (q_tok * 17 + 31) // 32
    matched = (expert_ids == expert).astype(jnp.int32)
    chosen = jnp.sum(matched, axis=1)
    weight = jnp.sum(gate_values * matched.astype(jnp.float32), axis=1)
    slot = jnp.cumsum(chosen) - chosen
    gain_row = -(-capacity // 8) * 8
    rows = jnp.arange(-(-(gain_row + 1) // 16) * 16, dtype=jnp.int32)[:, None]
    dispatch = (slot[None, :] == rows) & (rows < capacity) & (
        chosen[None, :] == 1
    )
    row_weight = jnp.sum(jnp.where(dispatch, weight[None, :], 0.0), axis=1, keepdims=True)
    dispatch = dispatch.astype(jnp.bfloat16)

    place = jnp.stack(
        [seq_at * ctx_dev, limit, seq_at, core, seq_at % run * quarter + exp_at // 2]
    )
    parts, later, dispatch, row_weight = attend(
        context,
        q_tok,
        place,
        near_query,
        far_query,
        rotated_cache,
        key_cache,
        value_cache,
        rotated_fresh,
        key_new,
        value_new,
        dispatch,
        row_weight,
    )

    parts = exchange(parts.reshape(plane, run, group + 2, HD), "seq", flat)
    parts = parts.astype(jnp.float32)
    maxima = parts[:, :, group, :group]
    totals = parts[:, :, group, group : 2 * group] + parts[:, :, group, 2 * group : 3 * group]
    top = jnp.max(maxima, axis=0)
    weights = jnp.exp(maxima - top)
    total = jnp.sum(weights * totals, axis=0)
    sums = jnp.sum(weights[..., None] * parts[:, :, :group, :], axis=0).astype(jnp.bfloat16)
    total_high = total.astype(jnp.bfloat16)
    total_low = (total - total_high.astype(jnp.float32)).astype(jnp.bfloat16)
    facts = jnp.concatenate(
        [top.astype(jnp.bfloat16).ravel(), total_high.ravel(), total_low.ravel()]
    )
    facts = jnp.pad(facts, (0, HD - facts.shape[0]))[None]
    lines = jnp.concatenate(
        [
            sums.reshape(run * group, HD),
            facts,
            norm_gain.reshape(group, HD),
            facts,
        ]
    )
    lines = spread(lines, ("seq", "exp"), run * quarter, tall)
    lines = lines.reshape(run, quarter, -1, HD)
    gain = lines[0, :, run * group + 1 : run * group + 1 + group]
    facts = lines[:, :, run * group, : 3 * run * group].astype(jnp.float32)
    facts = facts.reshape(run, quarter, 3, run, group)
    weights = jnp.exp(facts[:, :, 0] - jnp.max(facts[:, :, 0], axis=0))
    below = jnp.sum(weights * (facts[:, :, 1] + facts[:, :, 2]), axis=0)
    sums = lines[:, :, : run * group].astype(jnp.float32).reshape(run, quarter, run, group, HD)
    above = jnp.sum(weights[..., None] * sums, axis=0)
    attention = (above / below[..., None]).astype(jnp.bfloat16)
    attention = jnp.transpose(attention, (1, 0, 2, 3))

    tokens = spread(attention.reshape(run, quarter * group, HD), "seq", plane, flat)
    tokens = tokens.reshape(q_tok, quarter * width)
    gain = gain + dispatch[gain_row, 0] * tokens[0, 0]
    routed = dot(dispatch, tokens).astype(jnp.bfloat16)
    mine = jnp.concatenate(
        [routed[:gain_row], gain.reshape(1, quarter * width), routed[gain_row + 1 :]]
    )
    other = swap(mine, "exp", 1)
    kept, sent, own = feed(
        gain_row,
        later,
        mine,
        other,
        w_gate,
        w_up,
        w_down,
        attention.reshape(run * quarter, group, HD),
    )

    half = kept + swap(sent, "exp", 1).astype(jnp.float32)
    half = (half * row_weight).astype(jnp.bfloat16)
    rows = jnp.dot(dispatch.T, half, preferred_element_type=jnp.float32).astype(jnp.bfloat16)
    rows = exchange(rows.reshape(plane, run, quarter * group, HD), "seq", flat)
    rows = jnp.sum(rows.astype(jnp.float32), axis=0).astype(jnp.bfloat16)
    rows = exchange(rows.reshape(run * quarter, group, HD), ("seq", "exp"), tall)
    expert_rows = jnp.sum(rows.astype(jnp.float32), axis=0)
    return (own + expert_rows).astype(jnp.bfloat16).reshape(1, width)


def solution(mesh):
    in_specs = (
        P("seq", "exp"),
        P("seq", "exp"),
        P("seq", "exp"),
        P("seq", "exp"),
        P("seq", "exp"),
        P(),
        P("exp"),
        P(),
        P(),
        P(None, ("seq", "exp")),
        P(None, ("seq", "exp")),
        P(("seq", "exp"), None),
    )
    out_specs = P("seq", "exp")
    return jax.shard_map(local, mesh=mesh, in_specs=in_specs, out_specs=out_specs, check_vma=False)
```
